32 devices in a mesh: dp: 16 (over z, y, core), mp: 2 (over x).
Axes of the slice: x: 2, y: 2, z: 4, core: 2. Of those that a mesh axis runs over, the one named last changes fastest.
Arguments:
- tokens: bfloat16 [40960, 1024], P(('dp', 'mp')), may hold values from -6 to 6
- cotangent: bfloat16 [40960, 1024], P(('dp', 'mp')), may hold values from -6 to 6
- group_start: int32 [16], P('dp'), may hold values from 0 to 1, as said below
- band_index: int32 [16], P('dp'), may hold values from 0 to 15, as said below
- class_label: int32 [16], P('dp'), may hold values from 0 to 100
- time_table: float32 [16, 1024], replicated, may hold values from -1.5 to 1.5
- class_table: float32 [101, 1024], replicated, may hold values from -1.5 to 1.5
- modulation_weight: bfloat16 [2, 1024, 6, 1024], P(None, None, None, 'mp'), may hold values from -0.1875 to 0.1875
- modulation_bias: float32 [2, 6, 1024], P(None, None, 'mp'), may hold values from -0.8 to 0.8
- input_weight: bfloat16 [2, 1024, 3, 1024], P(None, None, None, 'mp'), may hold values from -0.1875 to 0.1875
- output_weight: bfloat16 [2, 1024, 1024], P(None, 'mp'), may hold values from -0.5 to 0.5
- space_offsets: float32 [16, 62], P('mp'), may hold values from -0.8 to 0.8
- time_offsets: float32 [16, 39], P('mp'), may hold values from -0.8 to 0.8
- up_weight: bfloat16 [2, 1024, 4096], P(None, None, 'mp'), may hold values from -0.1875 to 0.1875
- up_bias: float32 [2, 4096], P(None, 'mp'), may hold values from -0.8 to 0.8
- down_weight: bfloat16 [2, 4096, 1024], P(None, 'mp'), may hold values from -0.09375 to 0.09375
Outputs:
- result: float32 [40960, 1024], P(('dp', 'mp'))
- grad_tokens: float32 [40960, 1024], P(('dp', 'mp'))
- grad_modulation_weight: float32 [2, 1024, 6, 1024], P(None, None, None, 'mp')
- grad_modulation_bias: float32 [2, 6, 1024], P(None, None, 'mp')
- grad_input_weight: float32 [2, 1024, 3, 1024], P(None, None, None, 'mp')
- grad_output_weight: float32 [2, 1024, 1024], P(None, 'mp')
- grad_space_offsets: float32 [16, 62], P('mp')
- grad_time_offsets: float32 [16, 39], P('mp')
- grad_up_weight: float32 [2, 1024, 4096], P(None, None, 'mp')
- grad_up_bias: float32 [2, 4096], P(None, 'mp')
- grad_down_weight: float32 [2, 4096, 1024], P(None, 'mp')
The draws below stay inside these ranges and needn't reach their ends.
Inputs may be any that keep to these rules, and one draw needn't show every extreme that they name: `group_start`: 1 marks the first video of a group, 0 the others; a group runs up to the next 1. `band_index`: read only where group_start is 1.
All inputs are finite; a program needn't handle non-finite values.
Results may differ from the reference program's by a relative error of at most 0.04.
The reference program's roundings to bfloat16 on the way count: a program that leaves them out, or rounds other values in their place, can miss the bound.
Values may be sent and summed in bfloat16 or wider, within the bound.
A program may use at most 512 MiB of HBM per device.

```python
import jax
import jax.numpy as jnp
from jax import lax

D = 1024
HEADS = 16
HEAD = 64
FF = 4096
CLASSES = 101
BANDS = 16
FRAMES = 5
HEIGHT = 16
WIDTH = 32
VIDEO_TOKENS = 2560
TOKENS = 40960
N_DP = 16


def group_flags(key):
    key = jax.random.fold_in(key, 5)
    coins = jax.random.randint(key, (N_DP,), 0, 3)
    place = jnp.arange(N_DP, dtype=jnp.int32)
    middle = (N_DP - 1) // 2
    flags = jnp.where(coins == 0, 1, 0)
    flags = jnp.where(place == 0, 1, flags)
    flags = jnp.where(place == 1, 0, flags)
    flags = jnp.where(place == middle, 1, flags)
    flags = jnp.where(place == middle + 1, 0, flags)
    return flags.astype(jnp.int32)


def draw_group_start(key, part):
    return group_flags(key)


def draw_band_index(key, part):
    flags = group_flags(key)
    key = jax.random.fold_in(key, 7)
    first_key, second_key = jax.random.split(key)
    offset = jax.random.randint(first_key, (), 0, BANDS)
    number = jnp.cumsum(flags) - 1
    leading = (number * 5 + offset) % BANDS
    others = jax.random.randint(second_key, (N_DP,), 0, BANDS)
    return jnp.where(flags > 0, leading, others).astype(jnp.int32)


def set_ends(result, own_key, least, largest):
    spot = [jax.random.randint(jax.random.fold_in(own_key, axis), (), 0, length) for axis, length in enumerate(result.shape)]
    widest = result.shape.index(max(result.shape))
    next_to = spot[:widest] + [(spot[widest] + 1) % result.shape[widest]] + spot[widest + 1:]
    return result.at[tuple(spot)].set(least).at[tuple(next_to)].set(largest)


def level_of(stream_key, dims, cuts, smallest, top_value):
    gain, own = 1.0, jax.random.fold_in(stream_key, 6)
    for axis_at, blocks in cuts:
        heights = jnp.exp(jax.random.uniform(jax.random.fold_in(own, axis_at), (blocks,), jnp.float32, smallest / len(cuts), top_value / len(cuts)))
        gain = gain * jnp.repeat(heights, dims[axis_at] // blocks).reshape([-1 if axis == axis_at else 1 for axis in range(len(dims))])
    return gain


def gaussian(own_key, shape, deviation, most, pieces=(), kind=jnp.bfloat16):
    array = deviation * jax.random.normal(own_key, shape, jnp.float32)
    if pieces:
        array = array * level_of(own_key, shape, pieces, -0.22, 0.18)
    return jnp.clip(array, -most, most).astype(kind)


def setup_inputs(seed: int = 0) -> dict:
    seeds = jax.random.split(jax.random.key(seed), 17)
    return {
        "tokens": gaussian(seeds[0], (TOKENS, D), 1.0, 6.0, ((0, 32),)),
        "cotangent": gaussian(seeds[1], (TOKENS, D), 1.0, 6.0, ((0, 32),)),
        "group_start": draw_group_start(jax.random.fold_in(seeds[16], 71), 0),
        "band_index": draw_band_index(jax.random.fold_in(seeds[16], 71), 0),
        "class_label": set_ends(jax.random.randint(seeds[4], (N_DP,), 0, CLASSES), jax.random.fold_in(seeds[4], 1), 0, CLASSES - 1).astype(jnp.int32),
        "time_table": jnp.clip(jax.random.uniform(seeds[5], (BANDS, D), jnp.float32, -1.5, 1.5), -1.5, 1.5),
        "class_table": jnp.clip(jax.random.uniform(seeds[6], (CLASSES, D), jnp.float32, -1.5, 1.5), -1.5, 1.5),
        "modulation_weight": gaussian(seeds[7], (2, D, 6, D), D ** -0.5, 0.1875, ((3, 2),)),
        "modulation_bias": jnp.clip(jax.random.uniform(seeds[8], (2, 6, D), jnp.float32, -0.8, 0.8) * level_of(seeds[8], (2, 6, D), ((2, 2),), -0.4, 0.0), -0.8, 0.8),
        "input_weight": gaussian(seeds[9], (2, D, 3, HEADS * HEAD), D ** -0.5, 0.1875, ((3, 2),)),
        "output_weight": gaussian(seeds[10], (2, HEADS * HEAD, D), (HEADS * HEAD // 8) ** -0.5, 0.5, ((1, 2),)),
        "space_offsets": jnp.clip(jax.random.uniform(seeds[11], (HEADS, 62), jnp.float32, -0.8, 0.8) * level_of(seeds[11], (HEADS, 62), ((0, 2),), -0.4, 0.0), -0.8, 0.8),
        "time_offsets": jnp.clip(jax.random.uniform(seeds[12], (HEADS, 2 * FRAMES + 29), jnp.float32, -0.8, 0.8) * level_of(seeds[12], (HEADS, 2 * FRAMES + 29), ((0, 2),), -0.4, 0.0), -0.8, 0.8),
        "up_weight": gaussian(seeds[13], (2, D, FF), D ** -0.5, 0.1875, ((2, 2),)),
        "up_bias": jnp.clip(jax.random.uniform(seeds[14], (2, FF), jnp.float32, -0.8, 0.8) * level_of(seeds[14], (2, FF), ((1, 2),), -0.4, 0.0), -0.8, 0.8),
        "down_weight": gaussian(seeds[15], (2, FF, D), FF ** -0.5, 0.09375, ((1, 2),)),
    }


HIGH = lax.Precision.HIGHEST
EPSILON = 1e-06

@jax.custom_vjp
def low(v):
    return lax.optimization_barrier(v.astype(jnp.bfloat16)).astype(jnp.float32)

@jax.custom_vjp
def low_back(v):
    return v

def low_keep(v):
    return (low(v), None)

def low_pass(kept, grad):
    return (grad,)

def back_keep(v):
    return (v, None)

def back_low(kept, grad):
    return (low(grad),)
low.defvjp(low_keep, low_pass)
low_back.defvjp(back_keep, back_low)

def normalize(values):
    centred = values - lax.optimization_barrier(jnp.mean(values, axis=-1, keepdims=True))
    spread = lax.optimization_barrier(jnp.mean(centred * centred, axis=-1, keepdims=True))
    return centred * lax.rsqrt(spread + EPSILON)

def modulate(values, shift, scale):
    return normalize(values) * (1.0 + scale) + shift

def window_shape(layer):
    if layer == 0:
        return (1, 16, 16)
    return (FRAMES, 8, 8)

def to_windows(values, layer):
    chans = values.shape[-1]
    if layer == 0:
        grid = values.reshape(FRAMES, HEIGHT // 16, 16, WIDTH // 16, 16, chans)
        return grid.transpose(0, 1, 3, 2, 4, 5).reshape(-1, 256, chans)
    grid = values.reshape(FRAMES, HEIGHT // 8, 8, WIDTH // 8, 8, chans)
    return grid.transpose(1, 3, 0, 2, 4, 5).reshape(-1, FRAMES * 64, chans)

def from_windows(values, layer):
    chans = values.shape[-1]
    if layer == 0:
        grid = values.reshape(FRAMES, HEIGHT // 16, WIDTH // 16, 16, 16, chans)
        return grid.transpose(0, 1, 3, 2, 4, 5).reshape(-1, chans)
    grid = values.reshape(HEIGHT // 8, WIDTH // 8, FRAMES, 8, 8, chans)
    return grid.transpose(2, 0, 3, 1, 4, 5).reshape(-1, chans)

def offset_map(layer):
    extents = window_shape(layer)
    count = extents[0] * extents[1] * extents[2]
    place = jnp.arange(count, dtype=jnp.int32)
    positions = (place // (extents[1] * extents[2]), place // extents[2] % extents[1], place % extents[2])
    columns = []
    for position, extent in zip(positions, extents):
        if extent > 1:
            offset = (position[:, None] - position[None, :] + extent - 1).reshape(-1)
            levels = jnp.arange(2 * extent - 1, dtype=jnp.int32)
            columns.append((offset[:, None] == levels[None, :]).astype(jnp.float32))
    return jnp.concatenate(columns, axis=1)

def attend(projected, offsets, layer):
    windows = to_windows(projected, layer)
    count = windows.shape[1]
    split = windows.reshape(windows.shape[0], count, 3, HEADS, HEAD)
    queries = split[:, :, 0]
    keys = split[:, :, 1]
    values = split[:, :, 2]
    bias = jnp.dot(offsets, offset_map(layer).T, precision=HIGH).reshape(HEADS, count, count)
    scores = jnp.einsum('nqhe,nkhe->nhqk', queries, keys, precision=HIGH) * HEAD ** (-0.5) + bias
    scores = low_back(scores)
    probs = low(jax.nn.softmax(scores, axis=-1))
    mixed = jnp.einsum('nhqk,nkhe->nqhe', probs, values, precision=HIGH)
    return from_windows(mixed.reshape(mixed.shape[0], count, HEADS * HEAD), layer)

def block(values, modulation, input_weight, output_weight, offsets, up_weight, up_bias, down_weight, layer):
    normed = low(modulate(values, modulation[0], modulation[1]))
    projected = jnp.dot(normed, input_weight.reshape(input_weight.shape[0], -1), precision=HIGH)
    projected = low(low_back(projected))
    attended = low(low_back(attend(projected, offsets, layer)))
    branch = low_back(jnp.dot(attended, output_weight, precision=HIGH))
    middle = values + modulation[2] * branch
    normed_two = low(modulate(middle, modulation[3], modulation[4]))
    hidden_pre = low_back(jnp.dot(normed_two, up_weight, precision=HIGH) + up_bias)
    hidden = low(jax.nn.gelu(hidden_pre))
    branch_two = low_back(jnp.dot(hidden, down_weight, precision=HIGH))
    return middle + modulation[5] * branch_two

def video_forward(values, activated, params):
    modulation_weight, modulation_bias, input_weight, output_weight, space_offsets, time_offsets, up_weight, up_bias, down_weight = params
    modulation = jnp.einsum('d,ldcf->lcf', activated, modulation_weight, precision=HIGH) + modulation_bias
    tables = (space_offsets, time_offsets)
    for layer in range(2):
        values = block(values, modulation[layer], input_weight[layer], output_weight[layer], tables[layer], up_weight[layer], up_bias[layer], down_weight[layer], layer)
    return values

def reference(tokens, cotangent, group_start, band_index, class_label, time_table, class_table, modulation_weight, modulation_bias, input_weight, output_weight, space_offsets, time_offsets, up_weight, up_bias, down_weight):
    place = jnp.arange(N_DP, dtype=jnp.int32)
    heads_at = jnp.where(group_start > 0, place, -1).astype(jnp.int32)
    head_of = lax.cummax(heads_at, axis=0)
    band = band_index[head_of]
    activated = low(jax.nn.silu(time_table[band] + class_table[class_label]))
    params = (modulation_weight.astype(jnp.float32), modulation_bias.astype(jnp.float32), input_weight.astype(jnp.float32), output_weight.astype(jnp.float32), space_offsets.astype(jnp.float32), time_offsets.astype(jnp.float32), up_weight.astype(jnp.float32), up_bias.astype(jnp.float32), down_weight.astype(jnp.float32))
    videos = tokens.astype(jnp.float32).reshape(N_DP, VIDEO_TOKENS, D)
    upstreams = cotangent.astype(jnp.float32).reshape(N_DP, VIDEO_TOKENS, D)
    totals = tuple((jnp.zeros_like(param) for param in params))

    def one_video(carried, item):
        values, upstream, condition = item

        def forward(inputs, weights):
            return video_forward(inputs, condition, weights)
        output, pull = jax.vjp(forward, values, params)
        grad_values, grad_params = pull(upstream)
        return (jax.tree.map(jnp.add, carried, grad_params), (output, grad_values))
    totals, (outputs, grads) = lax.scan(one_video, totals, (videos, upstreams, activated))
    return (outputs.reshape(TOKENS, D), grads.reshape(TOKENS, D), totals[0], totals[1], totals[2], totals[3], totals[4], totals[5], totals[6], totals[7], totals[8])
```

```python
import functools

import jax
import jax.numpy as jnp
import numpy as np
from jax import lax
from jax.experimental import pallas as pl
from jax.experimental.pallas import tpu as pltpu
from jax.sharding import Mesh
from jax.sharding import PartitionSpec as P

FRAMES = 5
HEIGHT = 16
WIDTH = 32


HIGH = lax.Precision.HIGHEST
EPSILON = 1e-06
CONTRACT_LAST = (((1,), (1,)), ((), ()))
CONTRACT_FIRST = (((0,), (0,)), ((), ()))


def carried_in(value, axis, join, neutral):
    count, mine = (lax.axis_size(axis), lax.axis_index(axis))
    pieces = lax.all_gather(value, axis)
    total = jnp.full_like(value, 0) + jnp.asarray(neutral, value.dtype)

    def lap(position, total):
        longer = join(total, pieces[position])
        return jnp.where(position < mine, longer, total)

    return lax.fori_loop(0, count - 1, lap, total)


def as_sent(shard):
    return jax.tree.map(lambda a: a.astype(jnp.bfloat16) if a.dtype == jnp.float32 else a, shard)


def normalize(values):
    centred = values - jnp.mean(values, axis=-1, keepdims=True)
    spread = jnp.mean(centred * centred, axis=-1, keepdims=True)
    return centred * lax.rsqrt(spread + EPSILON)


def modulate(values, shift, scale):
    return normalize(values) * (1.0 + scale) + shift


def window_shape(layer):
    if layer == 0:
        return (1, 16, 16)
    return (FRAMES, 8, 8)


def to_windows(values, layer):
    chans = values.shape[-1]
    if layer == 0:
        grid = values.reshape(FRAMES, HEIGHT // 16, 16, WIDTH // 16, 16, chans)
        return grid.transpose(0, 1, 3, 2, 4, 5).reshape(-1, 256, chans)
    grid = values.reshape(FRAMES, HEIGHT // 8, 8, WIDTH // 8, 8, chans)
    return grid.transpose(1, 3, 0, 2, 4, 5).reshape(-1, FRAMES * 64, chans)


def from_windows(values, layer):
    chans = values.shape[-1]
    if layer == 0:
        grid = values.reshape(FRAMES, HEIGHT // 16, WIDTH // 16, 16, 16, chans)
        return grid.transpose(0, 1, 3, 2, 4, 5).reshape(-1, chans)
    grid = values.reshape(HEIGHT // 8, WIDTH // 8, FRAMES, 8, 8, chans)
    return grid.transpose(2, 0, 3, 1, 4, 5).reshape(-1, chans)


def offset_map(layer):
    extents = window_shape(layer)
    count = extents[0] * extents[1] * extents[2]
    place = jnp.arange(count, dtype=jnp.int32)
    positions = (
        place // (extents[1] * extents[2]),
        place // extents[2] % extents[1],
        place % extents[2],
    )
    columns = []
    for position, extent in zip(positions, extents):
        if extent > 1:
            offset = (position[:, None] - position[None, :] + extent - 1).reshape(-1)
            levels = jnp.arange(2 * extent - 1, dtype=jnp.int32)
            columns.append((offset[:, None] == levels[None, :]).astype(jnp.float32))
    return jnp.concatenate(columns, axis=1)


def window_scores(projected, offsets, onehot, layer):
    windows = to_windows(projected, layer)
    count = windows.shape[1]
    heads = offsets.shape[0]
    split = windows.reshape(windows.shape[0], count, 3, heads, -1)
    queries = split[:, :, 0]
    keys = split[:, :, 1]
    values = split[:, :, 2]
    factor = split.shape[-1] ** (-0.5)
    bias = jnp.dot(offsets, onehot.T, precision=HIGH).reshape(heads, count, count)
    scores = (
        jnp.einsum("nqhe,nkhe->nhqk", queries, keys, preferred_element_type=jnp.float32) * factor
        + bias
    )
    return (queries, keys, values, scores, factor)


def gather_rows(values):
    return lax.all_gather(values, "mp", axis=0, tiled=True)


def gather_grads(values):
    return lax.all_gather(values, "mp", axis=0, tiled=True)


def scatter_rows(source, weight, count):

    def term(start, size):
        return jnp.dot(source, weight, preferred_element_type=jnp.float32)

    return lax.psum_scatter(
        term(jnp.int32(0), count * lax.axis_size("mp")), "mp", scatter_dimension=0, tiled=True
    )


def scatter_back(source, weight, count):

    def term(start, size):
        return lax.dot_general(source, weight, CONTRACT_LAST, preferred_element_type=jnp.float32)

    return lax.psum_scatter(
        term(jnp.int32(0), count * lax.axis_size("mp")).astype(jnp.bfloat16),
        "mp",
        scatter_dimension=0,
        tiled=True,
    ).astype(jnp.float32)


def per_device(
    tokens,
    cotangent,
    group_start,
    band_index,
    class_label,
    time_table,
    class_table,
    modulation_weight,
    modulation_bias,
    input_weight,
    output_weight,
    space_offsets,
    time_offsets,
    up_weight,
    up_bias,
    down_weight,
):
    local_rows = tokens.shape[0]
    marked = jnp.where(group_start > 0, band_index, -1)

    def latest(earlier, later):
        return jnp.where(later >= 0, later, earlier)

    before = carried_in(marked, "dp", latest, jnp.full_like(marked, -1))
    current = jnp.where(group_start > 0, band_index, before)
    band_hot = (
        current[:, None] == jnp.arange(time_table.shape[0], dtype=jnp.int32)[None, :]
    ).astype(jnp.float32)
    class_hot = (
        class_label[:, None] == jnp.arange(class_table.shape[0], dtype=jnp.int32)[None, :]
    ).astype(jnp.float32)
    condition = jnp.dot(band_hot, time_table, precision=HIGH) + jnp.dot(
        class_hot, class_table, precision=HIGH
    )
    activated = jax.nn.silu(condition[0]).astype(jnp.bfloat16)
    local_modulation = (
        jnp.einsum("d,ldcf->lcf", activated, modulation_weight, preferred_element_type=jnp.float32)
        + modulation_bias
    )
    modulation = lax.all_gather(local_modulation, "mp", axis=2, tiled=True)
    tables = (space_offsets, time_offsets)
    width = input_weight.shape[1]
    residual = tokens.astype(jnp.float32)
    saved = []
    for layer in range(2):
        shift_one, scale_one, gate_one, shift_two, scale_two, gate_two = [
            modulation[layer, number] for number in range(6)
        ]
        onehot = offset_map(layer)
        entry = residual
        normed = modulate(entry, shift_one, scale_one).astype(jnp.bfloat16)
        gathered = gather_rows(normed)
        projected = jnp.dot(
            gathered, input_weight[layer].reshape(width, -1), preferred_element_type=jnp.float32
        ).astype(jnp.bfloat16)
        queries, keys, values, scores, factor = window_scores(
            projected, tables[layer], onehot, layer
        )
        top = jnp.max(scores, axis=-1, keepdims=True)
        expo = jnp.exp(scores - top)
        total = jnp.sum(expo, axis=-1, keepdims=True)
        probs = (expo / total).astype(jnp.bfloat16)
        mixed = jnp.einsum("nhqk,nkhe->nqhe", probs, values, preferred_element_type=jnp.float32)
        attended = from_windows(
            mixed.reshape(mixed.shape[0], mixed.shape[1], -1).astype(jnp.bfloat16), layer
        )
        branch = scatter_rows(attended, output_weight[layer], local_rows)
        middle = entry + gate_one * branch
        normed_two = modulate(middle, shift_two, scale_two).astype(jnp.bfloat16)
        gathered_two = gather_rows(normed_two)
        hidden_pre = (
            jnp.dot(gathered_two, up_weight[layer], preferred_element_type=jnp.float32)
            + up_bias[layer]
        )
        hidden = jax.nn.gelu(hidden_pre).astype(jnp.bfloat16)
        branch_two = scatter_rows(hidden, down_weight[layer], local_rows)
        residual = middle + gate_two * branch_two
        saved.append(
            (
                entry,
                normed,
                gathered,
                projected,
                top,
                total,
                attended,
                branch,
                middle,
                normed_two,
                gathered_two,
                hidden_pre,
                hidden,
                branch_two,
            )
        )
    grad = cotangent.astype(jnp.float32)
    collected = [None, None]
    for layer in (1, 0):
        (
            entry,
            normed,
            gathered,
            projected,
            top,
            total,
            attended,
            branch,
            middle,
            normed_two,
            gathered_two,
            hidden_pre,
            hidden,
            branch_two,
        ) = saved[layer]
        shift_one, scale_one, gate_one, shift_two, scale_two, gate_two = [
            modulation[layer, number] for number in range(6)
        ]
        onehot = offset_map(layer)
        grad_down_branch = (gate_two * grad).astype(jnp.bfloat16)
        gate_two_grad = jnp.sum(grad * branch_two, axis=0)
        full_down = gather_grads(grad_down_branch)
        grad_hidden = lax.dot_general(
            full_down, down_weight[layer], CONTRACT_LAST, preferred_element_type=jnp.float32
        )
        down_grad = lax.dot_general(
            hidden, full_down, CONTRACT_FIRST, preferred_element_type=jnp.float32
        )
        gelu_pull = jax.vjp(jax.nn.gelu, hidden_pre)[1]
        grad_pre = gelu_pull(grad_hidden)[0].astype(jnp.bfloat16)
        up_bias_grad = jnp.sum(grad_pre, axis=0, dtype=jnp.float32)
        up_grad = lax.dot_general(
            gathered_two, grad_pre, CONTRACT_FIRST, preferred_element_type=jnp.float32
        )
        grad_normed_two = scatter_back(grad_pre, up_weight[layer], local_rows)
        middle_pull = jax.vjp(modulate, middle, shift_two, scale_two)[1]
        grad_middle, shift_two_grad, scale_two_grad = middle_pull(grad_normed_two)
        grad_middle = grad + grad_middle
        grad_out_branch = (gate_one * grad_middle).astype(jnp.bfloat16)
        gate_one_grad = jnp.sum(grad_middle * branch, axis=0)
        full_out = gather_grads(grad_out_branch)
        grad_attended = lax.dot_general(
            full_out, output_weight[layer], CONTRACT_LAST, preferred_element_type=jnp.float32
        ).astype(jnp.bfloat16)
        out_grad = lax.dot_general(
            attended, full_out, CONTRACT_FIRST, preferred_element_type=jnp.float32
        )
        queries, keys, values, scores, factor = window_scores(
            projected, tables[layer], onehot, layer
        )
        probs = jnp.exp(scores - top) / total
        heads = tables[layer].shape[0]
        upstream = to_windows(grad_attended, layer).reshape(queries.shape)
        grad_probs = jnp.einsum(
            "nqhe,nkhe->nhqk", upstream, values, preferred_element_type=jnp.float32
        )
        inner = jnp.sum(probs * grad_probs, axis=-1, keepdims=True)
        grad_scores = (probs * (grad_probs - inner)).astype(jnp.bfloat16)
        offset_grad = jnp.dot(
            jnp.sum(grad_scores, axis=0, dtype=jnp.float32).reshape(heads, -1),
            onehot,
            precision=HIGH,
        )
        grad_queries = (
            jnp.einsum("nhqk,nkhe->nqhe", grad_scores, keys, preferred_element_type=jnp.float32)
            * factor
        ).astype(jnp.bfloat16)
        grad_keys = (
            jnp.einsum("nhqk,nqhe->nkhe", grad_scores, queries, preferred_element_type=jnp.float32)
            * factor
        ).astype(jnp.bfloat16)
        grad_values = jnp.einsum(
            "nhqk,nqhe->nkhe",
            probs.astype(jnp.bfloat16),
            upstream,
            preferred_element_type=jnp.float32,
        ).astype(jnp.bfloat16)
        stacked = jnp.stack([grad_queries, grad_keys, grad_values], axis=2)
        grad_projected = from_windows(
            stacked.reshape(stacked.shape[0], stacked.shape[1], -1), layer
        )
        in_grad = lax.dot_general(
            gathered, grad_projected, CONTRACT_FIRST, preferred_element_type=jnp.float32
        ).reshape(input_weight.shape[1:])
        grad_normed = scatter_back(
            grad_projected, input_weight[layer].reshape(width, -1), local_rows
        )
        entry_pull = jax.vjp(modulate, entry, shift_one, scale_one)[1]
        grad_entry, shift_one_grad, scale_one_grad = entry_pull(grad_normed)
        grad = grad_middle + grad_entry
        partial_rows = jnp.stack(
            [
                shift_one_grad,
                scale_one_grad,
                gate_one_grad,
                shift_two_grad,
                scale_two_grad,
                gate_two_grad,
            ]
        )
        modulation_grad = lax.psum_scatter(partial_rows, "mp", scatter_dimension=1, tiled=True)
        projection_grad = activated.astype(jnp.float32)[:, None, None] * modulation_grad[None]
        grads_here = (
            projection_grad,
            modulation_grad,
            in_grad,
            out_grad,
            offset_grad,
            up_grad,
            up_bias_grad,
            down_grad,
        )
        collected[layer] = grads_here
    summed = jax.tree.map(
        lambda part: part.astype(jnp.float32), lax.psum(as_sent(collected[0] + collected[1]), "dp")
    )
    collected = [summed[:8], summed[8:]]

    def stacked_pair(number):
        return jnp.stack([collected[0][number], collected[1][number]])

    return (
        residual,
        grad,
        stacked_pair(0),
        stacked_pair(1),
        stacked_pair(2),
        stacked_pair(3),
        collected[0][4],
        collected[1][4],
        stacked_pair(5),
        stacked_pair(6),
        stacked_pair(7),
    )


VMEM = 58 * 2**20
ROWS = 256
HEAD = 64


def full_block(*shape):
    return pl.BlockSpec(shape, lambda *_: (0,) * len(shape))


def once_block(*shape):
    return pl.BlockSpec(shape, lambda *_: (0,) * len(shape), pipeline_mode=pl.Buffered(1))


def params():
    return pltpu.CompilerParams(vmem_limit_bytes=VMEM)


def cost(flops, moved, exps=0):
    return pl.CostEstimate(flops=int(flops), bytes_accessed=int(moved), transcendentals=int(exps))


def shaped(*arrays):
    return sum(int(np.prod(a.shape)) * a.dtype.itemsize for a in arrays)


def row_norm(values):
    centred = values - jnp.mean(values, axis=-1, keepdims=True)
    spread = jnp.mean(centred * centred, axis=-1, keepdims=True)
    scale = lax.rsqrt(spread + EPSILON)
    return centred * scale, scale


def norm_back(values, grad, shift_scale):
    unit, inverse = row_norm(values)
    inner = grad * (1.0 + shift_scale)
    first = jnp.mean(inner, axis=-1, keepdims=True)
    second = jnp.mean(inner * unit, axis=-1, keepdims=True)
    pulled = inverse * (inner - first - unit * second)
    return (
        pulled,
        jnp.sum(grad, axis=0, keepdims=True),
        jnp.sum(grad * unit, axis=0, keepdims=True),
    )


def project_kernel(x_ref, shift_ref, scale_ref, weight_ref, turned_ref, out_ref, normed_ref):
    rows = x_ref.shape[0]

    @pl.when(pl.program_id(0) == 0)
    def _():
        for start in range(0, rows, ROWS):
            part = pl.ds(start, ROWS)
            unit, _ = row_norm(x_ref[part, :])
            value = (unit * (1.0 + scale_ref[...]) + shift_ref[...]).astype(jnp.bfloat16)
            normed_ref[part, :] = value
            turned_ref[:, part] = value.T

    for start in range(0, rows, ROWS):
        part = pl.ds(start, ROWS)
        out_ref[0, part, :] = jnp.dot(
            normed_ref[part, :], weight_ref[0], preferred_element_type=jnp.float32
        ).astype(jnp.bfloat16)


def project(x, shift, scale, weight):
    rows, width = x.shape
    count, _, cols = weight.shape
    outs = (
        jax.ShapeDtypeStruct((width, rows), jnp.bfloat16),
        jax.ShapeDtypeStruct((count, rows, cols), jnp.bfloat16),
    )
    return pl.pallas_call(
        project_kernel,
        out_shape=outs,
        grid=(count,),
        in_specs=[
            once_block(rows, width),
            full_block(1, width),
            full_block(1, width),
            pl.BlockSpec((1, width, cols), lambda q: (q, 0, 0)),
        ],
        out_specs=(
            full_block(width, rows),
            pl.BlockSpec((1, rows, cols), lambda q: (q, 0, 0)),
        ),
        scratch_shapes=[pltpu.VMEM((rows, width), jnp.bfloat16)],
        compiler_params=params(),
        cost_estimate=cost(2 * rows * width * cols * count, shaped(x, weight, *outs)),
        name="project",
    )(x, shift, scale, weight)


def pair_scores(kk, query, ublk):
    scores = lax.dot_general(
        kk, jnp.concatenate([query, ublk], axis=1), CONTRACT_LAST, preferred_element_type=jnp.float32
    )
    expo = jnp.exp(scores - jnp.max(scores, axis=0, keepdims=True))
    return expo * (1.0 / jnp.sum(expo, axis=0, keepdims=True))


def attend_kernel(proj_ref, ublk_ref, place_ref, out_ref):
    count = proj_ref.shape[1]
    heads = ublk_ref.shape[0]
    wide = heads * HEAD
    lane = lax.broadcasted_iota(jnp.int32, (count, 128), 1)
    place = place_ref[...]
    for pair in range(heads // 2):
        query = proj_ref[0, :, pair * 128 : pair * 128 + 128]
        key = proj_ref[0, :, wide + pair * 128 : wide + pair * 128 + 128]
        value = proj_ref[0, :, 2 * wide + pair * 128 : 2 * wide + pair * 128 + 128]
        turned = value.T
        kk = jnp.concatenate([key, place], axis=1)
        halves = []
        for half in range(2):
            mine = (lane < HEAD) if half == 0 else (lane >= HEAD)
            scaled = jnp.where(mine, query * HEAD**-0.5, 0.0).astype(jnp.bfloat16)
            probs = pair_scores(kk, scaled, ublk_ref[2 * pair + half]).astype(jnp.bfloat16)
            mixed = jnp.dot(turned, probs, preferred_element_type=jnp.float32)
            halves.append(mixed[half * HEAD : half * HEAD + HEAD])
        out_ref[:, pair * 128 : pair * 128 + 128] = (
            jnp.concatenate(halves, axis=0).astype(jnp.bfloat16).T
        )


def attend(proj, ublk, place):
    quarters, rows, cols = proj.shape
    count = place.shape[0]
    heads = ublk.shape[0] // quarters
    out = jax.ShapeDtypeStruct((rows, quarters * heads * HEAD), jnp.bfloat16)
    pairs = rows * count * heads * quarters
    return pl.pallas_call(
        attend_kernel,
        out_shape=out,
        grid=(quarters, rows // count),
        in_specs=[
            pl.BlockSpec((1, count, cols), lambda q, w: (q, w, 0)),
            pl.BlockSpec((heads, count, 128), lambda q, w: (q, 0, 0)),
            full_block(count, 128),
        ],
        out_specs=pl.BlockSpec((count, heads * HEAD), lambda q, w: (w, q)),
        compiler_params=params(),
        cost_estimate=cost(pairs * 768, shaped(proj, ublk, out), pairs),
        name="attend",
    )(proj, ublk, place)


def join_kernel(
    att_ref, weight_ref, x_ref, gate_ref, shift_ref, scale_ref, branch_ref, middle_ref, normed_ref, turned_ref
):
    branch = jnp.dot(att_ref[...], weight_ref[...], preferred_element_type=jnp.float32)
    branch_ref[...] = branch
    middle = x_ref[...] + gate_ref[...] * branch
    middle_ref[...] = middle
    unit, _ = row_norm(middle)
    normed = (unit * (1.0 + scale_ref[...]) + shift_ref[...]).astype(jnp.bfloat16)
    normed_ref[...] = normed
    turned_ref[...] = normed.T


def join(att, weight, x, gate, shift, scale):
    rows, width = x.shape
    outs = (
        jax.ShapeDtypeStruct((rows, width), jnp.float32),
        jax.ShapeDtypeStruct((rows, width), jnp.float32),
        jax.ShapeDtypeStruct((rows, width), jnp.bfloat16),
        jax.ShapeDtypeStruct((width, rows), jnp.bfloat16),
    )
    tile = pl.BlockSpec((ROWS, width), lambda i: (i, 0))
    return pl.pallas_call(
        join_kernel,
        out_shape=outs,
        grid=(rows // ROWS,),
        in_specs=[tile, once_block(width, width), tile] + [full_block(1, width)] * 3,
        out_specs=(tile, tile, tile, pl.BlockSpec((width, ROWS), lambda i: (0, i))),
        compiler_params=params(),
        cost_estimate=cost(2 * rows * width * width, shaped(att, weight, x, *outs)),
        name="join",
    )(att, weight, x, gate, shift, scale)


SLOPE = float(np.sqrt(2 / np.pi))


def up_kernel(normed_ref, weight_ref, bias_ref, pre_ref, hidden_ref):
    for start in range(0, normed_ref.shape[0], ROWS):
        part = pl.ds(start, ROWS)
        pre = (
            jnp.dot(normed_ref[part, :], weight_ref[0], preferred_element_type=jnp.float32)
            + bias_ref[0]
        )
        pre_ref[0, part, :] = pre
        bent = jnp.tanh(SLOPE * (pre + 0.044715 * (pre * pre * pre)))
        hidden_ref[0, part, :] = (pre * (0.5 * (1.0 + bent))).astype(jnp.bfloat16)


def up(normed, weight, bias):
    rows, width = normed.shape
    count, _, cols = weight.shape
    outs = (
        jax.ShapeDtypeStruct((count, rows, cols), jnp.float32),
        jax.ShapeDtypeStruct((count, rows, cols), jnp.bfloat16),
    )
    return pl.pallas_call(
        up_kernel,
        out_shape=outs,
        grid=(count,),
        in_specs=[
            once_block(rows, width),
            pl.BlockSpec((1, width, cols), lambda q: (q, 0, 0)),
            pl.BlockSpec((1, 1, cols), lambda q: (q, 0, 0)),
        ],
        out_specs=(
            pl.BlockSpec((1, rows, cols), lambda q: (q, 0, 0)),
            pl.BlockSpec((1, rows, cols), lambda q: (q, 0, 0)),
        ),
        compiler_params=params(),
        cost_estimate=cost(2 * rows * width * cols * count, shaped(normed, weight, *outs)),
        name="up",
    )(normed, weight, bias)


def down_kernel(hidden_ref, weight_ref, middle_ref, gate_ref, branch_ref, out_ref):
    total = jnp.dot(hidden_ref[0], weight_ref[0], preferred_element_type=jnp.float32)
    for quarter in range(1, hidden_ref.shape[0]):
        total += jnp.dot(hidden_ref[quarter], weight_ref[quarter], preferred_element_type=jnp.float32)
    branch_ref[...] = total
    out_ref[...] = middle_ref[...] + gate_ref[...] * total


def down(hidden, weight, middle, gate):
    rows, width = middle.shape
    count, cols, _ = weight.shape
    outs = (
        jax.ShapeDtypeStruct((rows, width), jnp.float32),
        jax.ShapeDtypeStruct((rows, width), jnp.float32),
    )
    tile = pl.BlockSpec((ROWS, width), lambda i: (i, 0))
    return pl.pallas_call(
        down_kernel,
        out_shape=outs,
        grid=(rows // ROWS,),
        in_specs=[
            pl.BlockSpec((count, ROWS, cols), lambda i: (0, i, 0)),
            once_block(count, cols, width),
            tile,
            full_block(1, width),
        ],
        out_specs=(tile, tile),
        compiler_params=params(),
        cost_estimate=cost(2 * rows * width * cols * count, shaped(hidden, weight, middle, *outs)),
        name="down",
    )(hidden, weight, middle, gate)


def feed_back_kernel(
    list_ref, gdb_ref, hidden_ref, pre_ref, turned_ref, down_ref, up_ref,
    down_grad_ref, up_grad_ref, bias_grad_ref, normed_grad_ref, gpre_ref,
):
    rows = gdb_ref.shape[0]
    first = (pl.program_id(0) == 0) & (pl.program_id(1) == 0)
    sums = jnp.zeros(bias_grad_ref.shape[1:], jnp.float32)
    for start in range(0, rows, ROWS):
        part = pl.ds(start, ROWS)
        grad_hidden = lax.dot_general(
            gdb_ref[part, :], down_ref[0], CONTRACT_LAST, preferred_element_type=jnp.float32
        )
        pre = pre_ref[0, part, :]
        square = pre * pre
        bent = jnp.tanh(SLOPE * (pre + 0.044715 * (pre * square)))
        slope = 0.5 * (1.0 + bent) + (0.5 * SLOPE) * pre * (1.0 - bent * bent) * (
            1.0 + (3 * 0.044715) * square
        )
        grad_pre = (grad_hidden * slope).astype(jnp.bfloat16)
        gpre_ref[part, :] = grad_pre
        sums += jnp.sum(grad_pre.astype(jnp.float32), axis=0, keepdims=True)
    bias_grad_ref[0] = sums
    down_grad_ref[0] = lax.dot_general(
        hidden_ref[0], gdb_ref[...], CONTRACT_FIRST, preferred_element_type=jnp.float32
    ).astype(jnp.bfloat16)
    up_grad_ref[0] = jnp.dot(
        turned_ref[...], gpre_ref[...], preferred_element_type=jnp.float32
    ).astype(jnp.bfloat16)

    def term(part):
        return lax.dot_general(
            gpre_ref[part, :], up_ref[0], CONTRACT_LAST, preferred_element_type=jnp.float32
        )

    @pl.when(first)
    def _():
        for start in range(0, rows, ROWS):
            part = pl.ds(start, ROWS)
            normed_grad_ref[part, :] = term(part)

    @pl.when(jnp.logical_not(first))
    def _():
        for start in range(0, rows, ROWS):
            part = pl.ds(start, ROWS)
            normed_grad_ref[part, :] += term(part)


def feed_back(quarters, gdb, hidden, pre, turned, down_weight, up_weight):
    rows, width = gdb.shape
    cols = hidden.shape[2]
    step = min(512, cols)
    picked = quarters.shape[0]
    outs = (
        jax.ShapeDtypeStruct((picked, cols, width), jnp.bfloat16),
        jax.ShapeDtypeStruct((picked, width, cols), jnp.bfloat16),
        jax.ShapeDtypeStruct((picked, 1, cols), jnp.float32),
        jax.ShapeDtypeStruct((rows, width), jnp.float32),
    )
    grid_spec = pltpu.PrefetchScalarGridSpec(
        num_scalar_prefetch=1,
        grid=(picked, cols // step),
        in_specs=[
            once_block(rows, width),
            pl.BlockSpec((1, rows, step), lambda q, j, s: (s[q], 0, j)),
            pl.BlockSpec((1, rows, step), lambda q, j, s: (s[q], 0, j)),
            once_block(width, rows),
            pl.BlockSpec((1, step, width), lambda q, j, s: (s[q], j, 0)),
            pl.BlockSpec((1, width, step), lambda q, j, s: (s[q], 0, j)),
        ],
        out_specs=(
            pl.BlockSpec((1, step, width), lambda q, j, s: (q, j, 0)),
            pl.BlockSpec((1, width, step), lambda q, j, s: (q, 0, j)),
            pl.BlockSpec((1, 1, step), lambda q, j, s: (q, 0, j)),
            full_block(rows, width),
        ),
        scratch_shapes=[pltpu.VMEM((rows, step), jnp.bfloat16)],
    )
    return pl.pallas_call(
        feed_back_kernel,
        out_shape=outs,
        grid_spec=grid_spec,
        compiler_params=params(),
        cost_estimate=cost(8 * rows * width * cols * picked, shaped(gdb, turned, *outs) + 12 * rows * cols * picked),
        name="feed_back",
    )(quarters, gdb, hidden, pre, turned, down_weight, up_weight)


def join_back_kernel(
    one_ref, two_ref, g_ref, middle_ref, branch_ref, att_ref, weight_ref, gate_ref, scale_ref,
    grad_middle_ref, grad_att_ref, weight_grad_ref, sums_ref, total_ref,
):
    pulled, shift_sum, scale_sum = norm_back(
        middle_ref[...], one_ref[...] + two_ref[...], scale_ref[...]
    )
    grad_middle = g_ref[...] + pulled
    grad_middle_ref[...] = grad_middle
    gate_sum = jnp.sum(grad_middle * branch_ref[...], axis=0, keepdims=True)
    grad_branch = (gate_ref[...] * grad_middle).astype(jnp.bfloat16)
    grad_att_ref[...] = lax.dot_general(
        grad_branch, weight_ref[...], CONTRACT_LAST, preferred_element_type=jnp.float32
    ).astype(jnp.bfloat16)
    weight_term = lax.dot_general(
        att_ref[...], grad_branch, CONTRACT_FIRST, preferred_element_type=jnp.float32
    )
    sums = jnp.concatenate([shift_sum, scale_sum, gate_sum], axis=0)
    step = pl.program_id(0)

    @pl.when(step == 0)
    def _():
        total_ref[...] = weight_term
        sums_ref[...] = sums

    @pl.when(step > 0)
    def _():
        total_ref[...] += weight_term
        sums_ref[...] += sums

    @pl.when(step == pl.num_programs(0) - 1)
    def _():
        weight_grad_ref[...] = total_ref[...].astype(jnp.bfloat16)


def join_back(one, two, g, middle, branch, att, weight, gate, scale):
    rows, width = g.shape
    outs = (
        jax.ShapeDtypeStruct((rows, width), jnp.float32),
        jax.ShapeDtypeStruct((rows, width), jnp.bfloat16),
        jax.ShapeDtypeStruct((width, width), jnp.bfloat16),
        jax.ShapeDtypeStruct((3, width), jnp.float32),
    )
    tile = pl.BlockSpec((ROWS, width), lambda i: (i, 0))
    return pl.pallas_call(
        join_back_kernel,
        out_shape=outs,
        grid=(rows // ROWS,),
        in_specs=[tile] * 6 + [once_block(width, width)] + [full_block(1, width)] * 2,
        out_specs=(tile, tile, full_block(width, width), full_block(3, width)),
        scratch_shapes=[pltpu.VMEM((width, width), jnp.float32)],
        compiler_params=params(),
        cost_estimate=cost(4 * rows * width * width, shaped(one, two, g, middle, branch, att, weight, *outs)),
        name="join_back",
    )(one, two, g, middle, branch, att, weight, gate, scale)


def attend_back_kernel(proj_ref, grad_ref, ublk_ref, place_ref, out_ref, table_ref):
    count = proj_ref.shape[1]
    heads = ublk_ref.shape[0]
    wide = heads * HEAD
    lane = lax.broadcasted_iota(jnp.int32, (count, 128), 1)
    place = place_ref[...]
    fresh = pl.program_id(1) == 0

    @pl.when(fresh)
    def _():
        table_ref[...] = jnp.zeros_like(table_ref)

    for pair in range(heads // 2):
        part = slice(pair * 128, pair * 128 + 128)
        query = proj_ref[0, :, part]
        key = proj_ref[0, :, wide + pair * 128 : wide + pair * 128 + 128]
        value = proj_ref[0, :, 2 * wide + pair * 128 : 2 * wide + pair * 128 + 128]
        upstream = grad_ref[:, part]
        turned = (key * HEAD**-0.5).astype(jnp.bfloat16).T
        kk = jnp.concatenate([key, place], axis=1)
        halves = []
        grad_key = jnp.zeros((count, 128), jnp.float32)
        grad_value = jnp.zeros((count, 128), jnp.float32)
        for half in range(2):
            mine = (lane < HEAD) if half == 0 else (lane >= HEAD)
            scaled = jnp.where(mine, query * HEAD**-0.5, 0.0).astype(jnp.bfloat16)
            above = jnp.where(mine, upstream, 0.0).astype(jnp.bfloat16)
            probs = pair_scores(kk, scaled, ublk_ref[2 * pair + half])
            grad_probs = lax.dot_general(
                value, above, CONTRACT_LAST, preferred_element_type=jnp.float32
            )
            inner = jnp.sum(probs * grad_probs, axis=0, keepdims=True)
            grad_scores = (probs * (grad_probs - inner)).astype(jnp.bfloat16)
            both = jnp.dot(
                grad_scores,
                jnp.concatenate([scaled, place], axis=1),
                preferred_element_type=jnp.float32,
            )
            grad_key += both[:, :128]
            table_ref[2 * pair + half] += both[:, 128:]
            grad_value += jnp.dot(
                probs.astype(jnp.bfloat16), above, preferred_element_type=jnp.float32
            )
            grad_query = jnp.dot(turned, grad_scores, preferred_element_type=jnp.float32)
            halves.append(grad_query[half * HEAD : half * HEAD + HEAD])
        out_ref[0, :, part] = jnp.concatenate(halves, axis=0).astype(jnp.bfloat16).T
        out_ref[0, :, wide + pair * 128 : wide + pair * 128 + 128] = grad_key.astype(jnp.bfloat16)
        out_ref[0, :, 2 * wide + pair * 128 : 2 * wide + pair * 128 + 128] = grad_value.astype(
            jnp.bfloat16
        )


def attend_back(proj, grad, ublk, place):
    quarters, rows, cols = proj.shape
    count = place.shape[0]
    heads = ublk.shape[0] // quarters
    outs = (
        jax.ShapeDtypeStruct(proj.shape, jnp.bfloat16),
        jax.ShapeDtypeStruct((ublk.shape[0], count, 128), jnp.float32),
    )
    pairs = rows * count * heads * quarters
    return pl.pallas_call(
        attend_back_kernel,
        out_shape=outs,
        grid=(quarters, rows // count),
        in_specs=[
            pl.BlockSpec((1, count, cols), lambda q, w: (q, w, 0)),
            pl.BlockSpec((count, heads * HEAD), lambda q, w: (w, q)),
            pl.BlockSpec((heads, count, 128), lambda q, w: (q, 0, 0)),
            full_block(count, 128),
        ],
        out_specs=(
            pl.BlockSpec((1, count, cols), lambda q, w: (q, w, 0)),
            pl.BlockSpec((heads, count, 128), lambda q, w: (q, 0, 0)),
        ),
        compiler_params=params(),
        cost_estimate=cost(pairs * 1536, shaped(proj, grad, ublk, *outs), pairs),
        name="attend_back",
    )(proj, grad, ublk, place)


def in_grad_kernel(list_ref, turned_ref, grad_ref, out_ref):
    out_ref[0] = jnp.dot(
        turned_ref[...], grad_ref[0], preferred_element_type=jnp.float32
    ).astype(jnp.bfloat16)


def in_grad(quarters, turned, grad):
    width, rows = turned.shape
    cols = grad.shape[2]
    picked = quarters.shape[0]
    out = jax.ShapeDtypeStruct((picked, width, cols), jnp.bfloat16)
    grid_spec = pltpu.PrefetchScalarGridSpec(
        num_scalar_prefetch=1,
        grid=(picked, 2),
        in_specs=[
            pl.BlockSpec((width // 2, rows), lambda q, j, s: (j, 0)),
            pl.BlockSpec((1, rows, cols), lambda q, j, s: (s[q], 0, 0)),
        ],
        out_specs=pl.BlockSpec((1, width // 2, cols), lambda q, j, s: (q, j, 0)),
    )
    return pl.pallas_call(
        in_grad_kernel,
        out_shape=out,
        grid_spec=grid_spec,
        compiler_params=params(),
        cost_estimate=cost(2 * rows * width * cols * picked, shaped(turned, out) + 2 * rows * cols * picked),
        name="in_grad",
    )(quarters, turned, grad)


def project_back_kernel(
    grad_ref, weight_ref, x_ref, middle_ref, scale_ref, out_ref, sums_ref
):
    total = lax.dot_general(
        grad_ref[0], weight_ref[0], CONTRACT_LAST, preferred_element_type=jnp.float32
    )
    for quarter in range(1, grad_ref.shape[0]):
        total += lax.dot_general(
            grad_ref[quarter], weight_ref[quarter], CONTRACT_LAST, preferred_element_type=jnp.float32
        )
    pulled, shift_sum, scale_sum = norm_back(x_ref[...], total, scale_ref[...])
    out_ref[...] = middle_ref[...] + pulled
    sums = jnp.concatenate([shift_sum, scale_sum], axis=0)

    @pl.when(pl.program_id(0) == 0)
    def _():
        sums_ref[...] = sums

    @pl.when(pl.program_id(0) > 0)
    def _():
        sums_ref[...] += sums


def project_back(grad, weight, x, grad_middle, scale):
    rows, width = x.shape
    count, _, cols = weight.shape
    outs = (
        jax.ShapeDtypeStruct((rows, width), jnp.float32),
        jax.ShapeDtypeStruct((2, width), jnp.float32),
    )
    tile = pl.BlockSpec((ROWS, width), lambda i: (i, 0))
    return pl.pallas_call(
        project_back_kernel,
        out_shape=outs,
        grid=(rows // ROWS,),
        in_specs=[
            pl.BlockSpec((count, ROWS, cols), lambda i: (0, i, 0)),
            once_block(count, width, cols),
            tile,
            tile,
            full_block(1, width),
        ],
        out_specs=(tile, full_block(2, width)),
        compiler_params=params(),
        cost_estimate=cost(2 * rows * width * cols * count, shaped(grad, weight, x, grad_middle, *outs)),
        name="project_back",
    )(grad, weight, x, grad_middle, scale)


SWAP = [(0, 1), (1, 0)]


def either(flag, one, two):
    return jnp.where(flag, one, two)


def split_bits(values):
    parts = []
    for _ in range(3):
        part = lax.reduce_precision(values, 8, 7)
        parts.append(part.astype(jnp.bfloat16))
        values = values - part
    return parts


def place_maps(layer, frames):
    extents = window_shape(layer)
    count = extents[0] * extents[1] * extents[2]
    place = np.arange(count)
    positions = (place // (extents[1] * extents[2]), place // extents[2] % extents[1], place % extents[2])
    hots = []
    width = sum(e for e in extents if e > 1)
    levels = sum(2 * e - 1 for e in extents if e > 1)
    pick = np.zeros((levels, width, width), np.float32)
    column = base = 0
    for position, extent in zip(positions, extents):
        if extent == 1:
            continue
        spots = jnp.asarray(position, jnp.int32)
        if extent == FRAMES and layer == 1:
            spots = frames[spots]
        hots.append((spots[:, None] == jnp.arange(extent, dtype=jnp.int32)[None, :]).astype(jnp.float32))
        for i in range(extent):
            for j in range(extent):
                pick[base + i - j + extent - 1, column + i, column + j] = 1
        column += extent
        base += 2 * extent - 1
    return jnp.concatenate(hots, axis=1), pick


def bias_blocks(table, hot, pick):
    pairs = jnp.einsum("hx,xij->hij", table, pick, precision=HIGH)
    spread = jnp.einsum("ai,hij->haj", hot, pairs, precision=HIGH)
    parts = split_bits(spread)
    room = 128 - 3 * hot.shape[1]
    padded = jnp.concatenate(parts + [jnp.zeros(spread.shape[:2] + (room,), jnp.bfloat16)], axis=2)
    one = hot.astype(jnp.bfloat16)
    place = jnp.concatenate([one] * 3 + [jnp.zeros((hot.shape[0], room), jnp.bfloat16)], axis=1)
    return padded, place


def table_grad(acc, hot, pick):
    width = hot.shape[1]
    pairs = jnp.einsum("hbi,bj->hij", acc[:, :, :width], hot, precision=HIGH)
    return jnp.einsum("hij,xij->hx", pairs, pick, precision=HIGH)


def per_device_pair(
    tokens,
    cotangent,
    group_start,
    band_index,
    class_label,
    time_table,
    class_table,
    modulation_weight,
    modulation_bias,
    input_weight,
    output_weight,
    space_offsets,
    time_offsets,
    up_weight,
    up_bias,
    down_weight,
):
    core = lax.axis_index("core")
    side = lax.axis_index("mp")
    dp = ("chip", "core")
    low_side = side == 0
    rows, width = tokens.shape
    bf16, f32 = jnp.bfloat16, jnp.float32

    def swap_side(value):
        return lax.ppermute(value, "mp", SWAP)

    def swap_core(value):
        return lax.ppermute(value, "core", SWAP)

    def half_of(value, axis):
        size = value.shape[axis] // 2
        return lax.dynamic_slice_in_dim(value, core * size, size, axis)

    def gather4(value):
        got = lax.all_gather(value, ("core", "mp"))
        return got.reshape((4,) + value.shape)

    weights = []
    for layer in range(2):
        in_piece = jnp.concatenate(
            [half_of(input_weight[layer, :, part], 1) for part in range(3)], axis=1
        )
        weights.append(
            (
                gather4(in_piece),
                gather4(half_of(output_weight[layer], 0)),
                gather4(half_of(up_weight[layer], 1)),
                gather4(half_of(down_weight[layer], 0)),
            )
        )
    heads = space_offsets.shape[0] // 2
    small_sizes = [heads * space_offsets.shape[1], heads * time_offsets.shape[1], up_bias.shape[1]]
    small = jnp.concatenate(
        [half_of(space_offsets, 0).reshape(-1), half_of(time_offsets, 0).reshape(-1), half_of(up_bias, 1).reshape(-1)]
    )
    small = gather4(small)
    cut_one, cut_two = small_sizes[0], small_sizes[0] + small_sizes[1]
    tables = (
        small[:, :cut_one].reshape(4 * heads, -1),
        small[:, cut_one:cut_two].reshape(4 * heads, -1),
    )
    biases = small[:, cut_two:].reshape(4, 2, 1, -1)

    marked = jnp.where(group_start > 0, band_index, -1)
    every = lax.all_gather(marked, dp, tiled=True)
    mine = lax.axis_index(dp)
    order = jnp.arange(every.shape[0], dtype=jnp.int32)
    latest = jnp.max(jnp.where((every >= 0) & (order <= mine), order, -1))
    current = jnp.sum(jnp.where(order == latest, every, 0)) + jnp.where(latest < 0, -1, 0)
    band_hot = (current == jnp.arange(time_table.shape[0], dtype=jnp.int32)).astype(f32)
    class_hot = (class_label[0] == jnp.arange(class_table.shape[0], dtype=jnp.int32)).astype(f32)
    condition = jnp.sum(band_hot[:, None] * time_table, axis=0) + jnp.sum(
        class_hot[:, None] * class_table, axis=0
    )
    activated = jax.nn.silu(condition).astype(bf16)
    local_modulation = (
        jnp.einsum("d,ldcf->lcf", activated, modulation_weight, preferred_element_type=f32)
        + modulation_bias
    )
    modulation = lax.all_gather(local_modulation, "mp", axis=2, tiled=True)
    every_activated = lax.all_gather(activated, dp)

    split = lax.dynamic_slice_in_dim(tokens, (1 - side) * (rows - ROWS), ROWS, 0).reshape(8, 2, 16, width)
    kept = lax.dynamic_index_in_dim(split, side, 1, keepdims=False)
    got = swap_side(lax.dynamic_index_in_dim(split, 1 - side, 1, keepdims=False))
    shared = jnp.concatenate([either(low_side, kept, got), either(low_side, got, kept)], axis=0)
    whole = lax.dynamic_slice_in_dim(tokens, side * ROWS, rows - ROWS, 0)
    whole = whole.reshape(2, 16, 2, 16, width).transpose(0, 2, 1, 3, 4)
    x = jnp.concatenate([whole.reshape(-1, width), shared.reshape(-1, width)], axis=0).astype(f32)

    chunks = cotangent.reshape(5, ROWS, width)
    got = swap_side(jnp.stack([chunks[1], chunks[3]]))
    ordered = jnp.concatenate(
        [
            jnp.stack(
                [
                    either(low_side, chunks[0], chunks[2]),
                    either(low_side, chunks[2], chunks[4]),
                    either(low_side, chunks[4], chunks[0]),
                ]
            ),
            got,
        ]
    )
    g = ordered.reshape(5, 8, 4, 8, width).transpose(2, 0, 1, 3, 4).reshape(rows, width).astype(f32)

    frames = jnp.where(
        low_side,
        jnp.asarray([0, 1, 2, 3, 4], jnp.int32),
        jnp.asarray([3, 4, 2, 0, 1], jnp.int32),
    )
    maps = [place_maps(layer, frames) for layer in range(2)]
    blocks = [bias_blocks(tables[layer], *maps[layer]) for layer in range(2)]

    saved = []
    for layer in range(2):
        w_in, w_out, w_up, w_down = weights[layer]
        w_out = w_out.reshape(width, width)
        shift_one, scale_one, gate_one, shift_two, scale_two, gate_two = [
            modulation[layer, number][None] for number in range(6)
        ]
        ublk, place = blocks[layer]
        turned, proj = project(x, shift_one, scale_one, w_in)
        att = attend(proj, ublk, place)
        branch, middle, normed_two, turned_two = join(att, w_out, x, gate_one, shift_two, scale_two)
        pre, hidden = up(normed_two, w_up, biases[:, layer])
        branch_two, out = down(hidden, w_down, middle, gate_two)
        saved.append((x, turned, proj, att, branch, middle, turned_two, pre, hidden, branch_two))
        if layer == 0:
            parts = out.reshape(5, 2, 128, width)
            kept = lax.dynamic_index_in_dim(parts, side, 1, keepdims=False)
            sent = lax.dynamic_index_in_dim(parts, 1 - side, 1, keepdims=False).astype(bf16)
            got = swap_side(sent).astype(f32)
            shared = jnp.stack([either(low_side, kept[4], got[4]), either(low_side, got[4], kept[4])])
            x = jnp.concatenate([kept[:4], shared, got[:4]])
            x = x.reshape(5, 2, 8, 2, 8, width).transpose(1, 3, 0, 2, 4, 5).reshape(rows, width)

    parts = out.reshape(2, 2, 5, 8, 8, width).transpose(2, 0, 3, 1, 4, 5).reshape(5, 2, 8, 16, width)
    got = swap_side(parts[3:])
    pair = jnp.stack([either(low_side, parts[:2], got), either(low_side, got, parts[:2])], axis=2)
    pair = pair.reshape(2, 2, 16, 16, width).transpose(0, 2, 1, 3, 4).reshape(-1, width)
    shared = parts[2].transpose(1, 0, 2, 3).reshape(-1, width)
    result = either(
        low_side, jnp.concatenate([pair, shared], axis=0), jnp.concatenate([shared, pair], axis=0)
    )

    here = core * 2
    there = (1 - core) * 2
    keep_list = jnp.stack([here + side, here + 1 - side]).astype(jnp.int32)
    send_list = jnp.stack([there + side, there + 1 - side]).astype(jnp.int32)

    def reduced(send, keep):
        got = swap_core(send)
        own = keep[0].astype(f32) + got[0].astype(f32)
        other = (keep[1].astype(f32) + got[1].astype(f32)).astype(bf16)
        return (own + swap_side(other).astype(f32)).astype(bf16)

    before = []

    def over_chips(*values):
        if before:
            values = lax.optimization_barrier((values, before[-1]))[0]
        before.append(lax.psum(values, "chip"))
        return before[-1]

    collected = [None, None]
    for layer in (1, 0):
        w_in, w_out, w_up, w_down = weights[layer]
        w_out = w_out.reshape(width, width)
        shift_one, scale_one, gate_one, shift_two, scale_two, gate_two = [
            modulation[layer, number][None] for number in range(6)
        ]
        ublk, place = blocks[layer]
        x, turned, proj, att, branch, middle, turned_two, pre, hidden, branch_two = saved[layer]
        gdb = (gate_two * g).astype(bf16)
        gate_two_grad = jnp.sum(g * branch_two, axis=0)
        down_send, up_send, bias_send, grad_one = feed_back(
            send_list, gdb, hidden, pre, turned_two, w_down, w_up
        )
        down_keep, up_keep, bias_keep, grad_two = feed_back(
            keep_list, gdb, hidden, pre, turned_two, w_down, w_up
        )
        down_sum = reduced(down_send, down_keep)
        up_sum = reduced(up_send, up_keep)
        down_sum, up_sum = over_chips(down_sum, up_sum)
        grad_middle, grad_att, out_grad, sums_two = join_back(
            grad_one, grad_two, g, middle, branch, att, w_out, gate_one, scale_two
        )
        out_pieces = out_grad.reshape(2, 2, -1, width)
        out_send = lax.dynamic_index_in_dim(out_pieces, 1 - core, 0, keepdims=False)
        out_keep = lax.dynamic_index_in_dim(out_pieces, core, 0, keepdims=False)
        out_send = either(low_side, out_send, out_send[::-1])
        out_keep = either(low_side, out_keep, out_keep[::-1])
        out_sum = reduced(out_send, out_keep)
        grad_proj, acc = attend_back(proj, grad_att, ublk, place)
        in_sum = reduced(in_grad(send_list, turned, grad_proj), in_grad(keep_list, turned, grad_proj))
        out_sum, in_sum = over_chips(out_sum, in_sum)
        offset_grad = table_grad(acc, *maps[layer])
        g, sums_one = project_back(grad_proj, w_in, x, grad_middle, scale_one)
        table_rows = jnp.stack(
            [sums_one[0], sums_one[1], sums_two[2], sums_two[0], sums_two[1], gate_two_grad]
        )
        if layer == 1:
            parts = g.reshape(2, 2, 5, 8, 8, width).transpose(2, 0, 3, 1, 4, 5).reshape(5, 2, 128, width)
            kept = jnp.concatenate(
                [parts[:2].reshape(4, 128, width), either(low_side, parts[2, 0], parts[2, 1])[None]]
            )
            sent = jnp.concatenate(
                [parts[3:].reshape(4, 128, width), either(low_side, parts[2, 1], parts[2, 0])[None]]
            )
            got = swap_side(sent.astype(bf16)).astype(f32)
            g = jnp.stack([either(low_side, kept, got), either(low_side, got, kept)], axis=1)
            g = g.reshape(rows, width)
        bias_rows = jnp.zeros((2, 2, bias_keep.shape[2]), f32)
        bias_rows = lax.dynamic_update_slice_in_dim(
            bias_rows, either(low_side, bias_keep[:, 0], bias_keep[::-1, 0])[None], core, 0
        )
        bias_rows = lax.dynamic_update_slice_in_dim(
            bias_rows, either(low_side, bias_send[:, 0], bias_send[::-1, 0])[None], 1 - core, 0
        )
        half = width // 2
        by_side = [
            jnp.concatenate(
                [
                    table_rows[:, s * half : s * half + half].reshape(-1),
                    offset_grad.reshape(2, 2, -1)[:, s].reshape(-1),
                    bias_rows[:, s].reshape(-1),
                ]
            )
            for s in range(2)
        ]
        summed = either(low_side, by_side[0], by_side[1]) + swap_side(
            either(low_side, by_side[1], by_side[0])
        )
        spread = lax.all_gather(summed, dp)
        row_part = spread[:, : 6 * half].reshape(-1, 6, half)
        rest = jnp.sum(spread[:, 6 * half :], axis=0)
        offsets_size = offset_grad.size // 2
        offset_sum = rest[:offsets_size].reshape(2 * heads, -1)
        bias_sum = rest[offsets_size:]
        weight_rows = jnp.einsum(
            "vd,vcf->dcf", every_activated.astype(f32), row_part, precision=HIGH
        )
        collected[layer] = (
            weight_rows,
            jnp.sum(row_part, axis=0),
            (in_sum, out_sum, up_sum, down_sum),
            offset_sum,
            bias_sum,
        )

    parts = g.reshape(5, 2, 128, width)
    kept = lax.dynamic_index_in_dim(parts[4], side, 0, keepdims=False).reshape(8, 16, width)
    sent = lax.dynamic_index_in_dim(parts[4], 1 - side, 0, keepdims=False).reshape(8, 16, width)
    got = swap_side(sent)
    shared = jnp.stack([either(low_side, kept, got), either(low_side, got, kept)], axis=1).reshape(-1, width)
    whole = parts[:4].reshape(2, 2, 16, 16, width).transpose(0, 2, 1, 3, 4).reshape(-1, width)
    grad_tokens = either(
        low_side, jnp.concatenate([whole, shared], axis=0), jnp.concatenate([shared, whole], axis=0)
    )

    first_core = core == 0

    def whole_of(value, axis):
        other = swap_core(value)
        return jnp.concatenate(
            [either(first_core, value, other), either(first_core, other, value)], axis=axis
        ).astype(f32)

    def pair_of(number, axis, shape=None):
        both = []
        for layer in range(2):
            value = collected[layer][2][number]
            if shape is not None:
                value = value.reshape(shape)
            both.append(whole_of(value, axis))
        return jnp.stack(both)

    return (
        result,
        grad_tokens,
        jnp.stack([collected[0][0], collected[1][0]]),
        jnp.stack([collected[0][1], collected[1][1]]),
        pair_of(0, 2, (width, 3, -1)),
        pair_of(1, 0),
        collected[0][3],
        collected[1][3],
        pair_of(2, 1),
        jnp.stack([collected[0][4], collected[1][4]]),
        pair_of(3, 0),
    )


def solution(mesh):
    if mesh.shape["mp"] == 2 and mesh.shape["dp"] % 2 == 0:
        dp, run = ("chip", "core"), per_device_pair
        mesh = Mesh(mesh.devices.reshape(-1, 2, 2), ("chip", "core", "mp"))
    else:
        dp, run = ("dp",), per_device
    both = dp + ("mp",)
    return jax.shard_map(
        run,
        mesh=mesh,
        in_specs=(
            P(both, None),
            P(both, None),
            P(dp),
            P(dp),
            P(dp),
            P(),
            P(),
            P(None, None, None, "mp"),
            P(None, None, "mp"),
            P(None, None, None, "mp"),
            P(None, "mp", None),
            P("mp", None),
            P("mp", None),
            P(None, None, "mp"),
            P(None, "mp"),
            P(None, "mp", None),
        ),
        out_specs=(
            P(both, None),
            P(both, None),
            P(None, None, None, "mp"),
            P(None, None, "mp"),
            P(None, None, None, "mp"),
            P(None, "mp", None),
            P("mp", None),
            P("mp", None),
            P(None, None, "mp"),
            P(None, "mp"),
            P(None, "mp", None),
        ),
        check_vma=False,
    )
```

```python
import functools

import jax
import jax.numpy as jnp
import numpy as np
from jax import lax
from jax.experimental import pallas as pl
from jax.experimental.pallas import tpu as pltpu
from jax.sharding import Mesh
from jax.sharding import PartitionSpec as P

FRAMES = 5
HEIGHT = 16
WIDTH = 32


HIGH = lax.Precision.HIGHEST
EPSILON = 1e-06
CONTRACT_LAST = (((1,), (1,)), ((), ()))
CONTRACT_FIRST = (((0,), (0,)), ((), ()))


def carried_in(value, axis, join, neutral):
    count, mine = (lax.axis_size(axis), lax.axis_index(axis))
    pieces = lax.all_gather(value, axis)
    total = jnp.full_like(value, 0) + jnp.asarray(neutral, value.dtype)

    def lap(position, total):
        longer = join(total, pieces[position])
        return jnp.where(position < mine, longer, total)

    return lax.fori_loop(0, count - 1, lap, total)


def as_sent(shard):
    return jax.tree.map(lambda a: a.astype(jnp.bfloat16) if a.dtype == jnp.float32 else a, shard)


def normalize(values):
    centred = values - jnp.mean(values, axis=-1, keepdims=True)
    spread = jnp.mean(centred * centred, axis=-1, keepdims=True)
    return centred * lax.rsqrt(spread + EPSILON)


def modulate(values, shift, scale):
    return normalize(values) * (1.0 + scale) + shift


def window_shape(layer):
    if layer == 0:
        return (1, 16, 16)
    return (FRAMES, 8, 8)


def to_windows(values, layer):
    chans = values.shape[-1]
    if layer == 0:
        grid = values.reshape(FRAMES, HEIGHT // 16, 16, WIDTH // 16, 16, chans)
        return grid.transpose(0, 1, 3, 2, 4, 5).reshape(-1, 256, chans)
    grid = values.reshape(FRAMES, HEIGHT // 8, 8, WIDTH // 8, 8, chans)
    return grid.transpose(1, 3, 0, 2, 4, 5).reshape(-1, FRAMES * 64, chans)


def from_windows(values, layer):
    chans = values.shape[-1]
    if layer == 0:
        grid = values.reshape(FRAMES, HEIGHT // 16, WIDTH // 16, 16, 16, chans)
        return grid.transpose(0, 1, 3, 2, 4, 5).reshape(-1, chans)
    grid = values.reshape(HEIGHT // 8, WIDTH // 8, FRAMES, 8, 8, chans)
    return grid.transpose(2, 0, 3, 1, 4, 5).reshape(-1, chans)


def offset_map(layer):
    extents = window_shape(layer)
    count = extents[0] * extents[1] * extents[2]
    place = jnp.arange(count, dtype=jnp.int32)
    positions = (
        place // (extents[1] * extents[2]),
        place // extents[2] % extents[1],
        place % extents[2],
    )
    columns = []
    for position, extent in zip(positions, extents):
        if extent > 1:
            offset = (position[:, None] - position[None, :] + extent - 1).reshape(-1)
            levels = jnp.arange(2 * extent - 1, dtype=jnp.int32)
            columns.append((offset[:, None] == levels[None, :]).astype(jnp.float32))
    return jnp.concatenate(columns, axis=1)


def window_scores(projected, offsets, onehot, layer):
    windows = to_windows(projected, layer)
    count = windows.shape[1]
    heads = offsets.shape[0]
    split = windows.reshape(windows.shape[0], count, 3, heads, -1)
    queries = split[:, :, 0]
    keys = split[:, :, 1]
    values = split[:, :, 2]
    factor = split.shape[-1] ** (-0.5)
    bias = jnp.dot(offsets, onehot.T, precision=HIGH).reshape(heads, count, count)
    scores = (
        jnp.einsum("nqhe,nkhe->nhqk", queries, keys, preferred_element_type=jnp.float32) * factor
        + bias
    )
    return (queries, keys, values, scores, factor)


def gather_rows(values):
    return lax.all_gather(values, "mp", axis=0, tiled=True)


def gather_grads(values):
    return lax.all_gather(values, "mp", axis=0, tiled=True)


def scatter_rows(source, weight, count):

    def term(start, size):
        return jnp.dot(source, weight, preferred_element_type=jnp.float32)

    return lax.psum_scatter(
        term(jnp.int32(0), count * lax.axis_size("mp")), "mp", scatter_dimension=0, tiled=True
    )


def scatter_back(source, weight, count):

    def term(start, size):
        return lax.dot_general(source, weight, CONTRACT_LAST, preferred_element_type=jnp.float32)

    return lax.psum_scatter(
        term(jnp.int32(0), count * lax.axis_size("mp")).astype(jnp.bfloat16),
        "mp",
        scatter_dimension=0,
        tiled=True,
    ).astype(jnp.float32)


def per_device(
    tokens,
    cotangent,
    group_start,
    band_index,
    class_label,
    time_table,
    class_table,
    modulation_weight,
    modulation_bias,
    input_weight,
    output_weight,
    space_offsets,
    time_offsets,
    up_weight,
    up_bias,
    down_weight,
):
    local_rows = tokens.shape[0]
    marked = jnp.where(group_start > 0, band_index, -1)

    def latest(earlier, later):
        return jnp.where(later >= 0, later, earlier)

    before = carried_in(marked, "dp", latest, jnp.full_like(marked, -1))
    current = jnp.where(group_start > 0, band_index, before)
    band_hot = (
        current[:, None] == jnp.arange(time_table.shape[0], dtype=jnp.int32)[None, :]
    ).astype(jnp.float32)
    class_hot = (
        class_label[:, None] == jnp.arange(class_table.shape[0], dtype=jnp.int32)[None, :]
    ).astype(jnp.float32)
    condition = jnp.dot(band_hot, time_table, precision=HIGH) + jnp.dot(
        class_hot, class_table, precision=HIGH
    )
    activated = jax.nn.silu(condition[0]).astype(jnp.bfloat16)
    local_modulation = (
        jnp.einsum("d,ldcf->lcf", activated, modulation_weight, preferred_element_type=jnp.float32)
        + modulation_bias
    )
    modulation = lax.all_gather(local_modulation, "mp", axis=2, tiled=True)
    tables = (space_offsets, time_offsets)
    width = input_weight.shape[1]
    residual = tokens.astype(jnp.float32)
    saved = []
    for layer in range(2):
        shift_one, scale_one, gate_one, shift_two, scale_two, gate_two = [
            modulation[layer, number] for number in range(6)
        ]
        onehot = offset_map(layer)
        entry = residual
        normed = modulate(entry, shift_one, scale_one).astype(jnp.bfloat16)
        gathered = gather_rows(normed)
        projected = jnp.dot(
            gathered, input_weight[layer].reshape(width, -1), preferred_element_type=jnp.float32
        ).astype(jnp.bfloat16)
        queries, keys, values, scores, factor = window_scores(
            projected, tables[layer], onehot, layer
        )
        top = jnp.max(scores, axis=-1, keepdims=True)
        expo = jnp.exp(scores - top)
        total = jnp.sum(expo, axis=-1, keepdims=True)
        probs = (expo / total).astype(jnp.bfloat16)
        mixed = jnp.einsum("nhqk,nkhe->nqhe", probs, values, preferred_element_type=jnp.float32)
        attended = from_windows(
            mixed.reshape(mixed.shape[0], mixed.shape[1], -1).astype(jnp.bfloat16), layer
        )
        branch = scatter_rows(attended, output_weight[layer], local_rows)
        middle = entry + gate_one * branch
        normed_two = modulate(middle, shift_two, scale_two).astype(jnp.bfloat16)
        gathered_two = gather_rows(normed_two)
        hidden_pre = (
            jnp.dot(gathered_two, up_weight[layer], preferred_element_type=jnp.float32)
            + up_bias[layer]
        )
        hidden = jax.nn.gelu(hidden_pre).astype(jnp.bfloat16)
        branch_two = scatter_rows(hidden, down_weight[layer], local_rows)
        residual = middle + gate_two * branch_two
        saved.append(
            (
                entry,
                normed,
                gathered,
                projected,
                top,
                total,
                attended,
                branch,
                middle,
                normed_two,
                gathered_two,
                hidden_pre,
                hidden,
                branch_two,
            )
        )
    grad = cotangent.astype(jnp.float32)
    collected = [None, None]
    for layer in (1, 0):
        (
            entry,
            normed,
            gathered,
            projected,
            top,
            total,
            attended,
            branch,
            middle,
            normed_two,
            gathered_two,
            hidden_pre,
            hidden,
            branch_two,
        ) = saved[layer]
        shift_one, scale_one, gate_one, shift_two, scale_two, gate_two = [
            modulation[layer, number] for number in range(6)
        ]
        onehot = offset_map(layer)
        grad_down_branch = (gate_two * grad).astype(jnp.bfloat16)
        gate_two_grad = jnp.sum(grad * branch_two, axis=0)
        full_down = gather_grads(grad_down_branch)
        grad_hidden = lax.dot_general(
            full_down, down_weight[layer], CONTRACT_LAST, preferred_element_type=jnp.float32
        )
        down_grad = lax.dot_general(
            hidden, full_down, CONTRACT_FIRST, preferred_element_type=jnp.float32
        )
        gelu_pull = jax.vjp(jax.nn.gelu, hidden_pre)[1]
        grad_pre = gelu_pull(grad_hidden)[0].astype(jnp.bfloat16)
        up_bias_grad = jnp.sum(grad_pre, axis=0, dtype=jnp.float32)
        up_grad = lax.dot_general(
            gathered_two, grad_pre, CONTRACT_FIRST, preferred_element_type=jnp.float32
        )
        grad_normed_two = scatter_back(grad_pre, up_weight[layer], local_rows)
        middle_pull = jax.vjp(modulate, middle, shift_two, scale_two)[1]
        grad_middle, shift_two_grad, scale_two_grad = middle_pull(grad_normed_two)
        grad_middle = grad + grad_middle
        grad_out_branch = (gate_one * grad_middle).astype(jnp.bfloat16)
        gate_one_grad = jnp.sum(grad_middle * branch, axis=0)
        full_out = gather_grads(grad_out_branch)
        grad_attended = lax.dot_general(
            full_out, output_weight[layer], CONTRACT_LAST, preferred_element_type=jnp.float32
        ).astype(jnp.bfloat16)
        out_grad = lax.dot_general(
            attended, full_out, CONTRACT_FIRST, preferred_element_type=jnp.float32
        )
        queries, keys, values, scores, factor = window_scores(
            projected, tables[layer], onehot, layer
        )
        probs = jnp.exp(scores - top) / total
        heads = tables[layer].shape[0]
        upstream = to_windows(grad_attended, layer).reshape(queries.shape)
        grad_probs = jnp.einsum(
            "nqhe,nkhe->nhqk", upstream, values, preferred_element_type=jnp.float32
        )
        inner = jnp.sum(probs * grad_probs, axis=-1, keepdims=True)
        grad_scores = (probs * (grad_probs - inner)).astype(jnp.bfloat16)
        offset_grad = jnp.dot(
            jnp.sum(grad_scores, axis=0, dtype=jnp.float32).reshape(heads, -1),
            onehot,
            precision=HIGH,
        )
        grad_queries = (
            jnp.einsum("nhqk,nkhe->nqhe", grad_scores, keys, preferred_element_type=jnp.float32)
            * factor
        ).astype(jnp.bfloat16)
        grad_keys = (
            jnp.einsum("nhqk,nqhe->nkhe", grad_scores, queries, preferred_element_type=jnp.float32)
            * factor
        ).astype(jnp.bfloat16)
        grad_values = jnp.einsum(
            "nhqk,nqhe->nkhe",
            probs.astype(jnp.bfloat16),
            upstream,
            preferred_element_type=jnp.float32,
        ).astype(jnp.bfloat16)
        stacked = jnp.stack([grad_queries, grad_keys, grad_values], axis=2)
        grad_projected = from_windows(
            stacked.reshape(stacked.shape[0], stacked.shape[1], -1), layer
        )
        in_grad = lax.dot_general(
            gathered, grad_projected, CONTRACT_FIRST, preferred_element_type=jnp.float32
        ).reshape(input_weight.shape[1:])
        grad_normed = scatter_back(
            grad_projected, input_weight[layer].reshape(width, -1), local_rows
        )
        entry_pull = jax.vjp(modulate, entry, shift_one, scale_one)[1]
        grad_entry, shift_one_grad, scale_one_grad = entry_pull(grad_normed)
        grad = grad_middle + grad_entry
        partial_rows = jnp.stack(
            [
                shift_one_grad,
                scale_one_grad,
                gate_one_grad,
                shift_two_grad,
                scale_two_grad,
                gate_two_grad,
            ]
        )
        modulation_grad = lax.psum_scatter(partial_rows, "mp", scatter_dimension=1, tiled=True)
        projection_grad = activated.astype(jnp.float32)[:, None, None] * modulation_grad[None]
        grads_here = (
            projection_grad,
            modulation_grad,
            in_grad,
            out_grad,
            offset_grad,
            up_grad,
            up_bias_grad,
            down_grad,
        )
        collected[layer] = grads_here
    summed = jax.tree.map(
        lambda part: part.astype(jnp.float32), lax.psum(as_sent(collected[0] + collected[1]), "dp")
    )
    collected = [summed[:8], summed[8:]]

    def stacked_pair(number):
        return jnp.stack([collected[0][number], collected[1][number]])

    return (
        residual,
        grad,
        stacked_pair(0),
        stacked_pair(1),
        stacked_pair(2),
        stacked_pair(3),
        collected[0][4],
        collected[1][4],
        stacked_pair(5),
        stacked_pair(6),
        stacked_pair(7),
    )


VMEM = 58 * 2**20
COST_SHARE = 64
ROWS = 256
HEAD = 64


def full_block(*shape):
    return pl.BlockSpec(shape, lambda *_: (0,) * len(shape))


def once_block(*shape):
    return pl.BlockSpec(shape, lambda *_: (0,) * len(shape), pipeline_mode=pl.Buffered(1))


def params():
    return pltpu.CompilerParams(vmem_limit_bytes=VMEM)


def cost(flops, moved, exps=0):
    return pl.CostEstimate(
        flops=int(flops) // COST_SHARE,
        bytes_accessed=int(moved) // COST_SHARE,
        transcendentals=int(exps) // COST_SHARE,
    )


def shaped(*arrays):
    return sum(int(np.prod(a.shape)) * a.dtype.itemsize for a in arrays)


def row_norm(values):
    centred = values - jnp.mean(values, axis=-1, keepdims=True)
    spread = jnp.mean(centred * centred, axis=-1, keepdims=True)
    scale = lax.rsqrt(spread + EPSILON)
    return centred * scale, scale


def norm_back(values, grad, shift_scale):
    unit, inverse = row_norm(values)
    inner = grad * (1.0 + shift_scale)
    first = jnp.mean(inner, axis=-1, keepdims=True)
    second = jnp.mean(inner * unit, axis=-1, keepdims=True)
    pulled = inverse * (inner - first - unit * second)
    return (
        pulled,
        jnp.sum(grad, axis=0, keepdims=True),
        jnp.sum(grad * unit, axis=0, keepdims=True),
    )


def call(kernel, name, grid, in_specs, out_specs, out_shape, flops, exps=0, scratch=()):
    def run(spots, *operands):
        moved = shaped(*operands, *jax.tree.leaves(out_shape))
        return pl.pallas_call(
            kernel,
            out_shape=out_shape,
            grid_spec=pltpu.PrefetchScalarGridSpec(
                num_scalar_prefetch=1,
                grid=grid,
                in_specs=in_specs,
                out_specs=out_specs,
                scratch_shapes=scratch,
            ),
            compiler_params=params(),
            cost_estimate=cost(flops, min(moved, 64 * 2**20), exps),
            name=name,
        )(spots, *operands)

    return run


def project_kernel(_, x_ref, shift_ref, scale_ref, weight_ref, turned_ref, normed_ref, out_ref):
    rows = x_ref.shape[0]

    @pl.when(pl.program_id(0) == 0)
    def _():
        for start in range(0, rows, ROWS):
            part = pl.ds(start, ROWS)
            unit, _ = row_norm(x_ref[part, :])
            value = (unit * (1.0 + scale_ref[...]) + shift_ref[...]).astype(jnp.bfloat16)
            normed_ref[part, :] = value
            turned_ref[:, part] = value.T

    project_rows(normed_ref, weight_ref, out_ref)


def side_by_side(ref):
    return jnp.concatenate([ref[0, part] for part in range(3)], axis=1)


def project_more_kernel(_, normed_ref, mine_ref, sib_ref, out_ref):
    @pl.when(pl.program_id(0) == 0)
    def _():
        project_rows(normed_ref, mine_ref, out_ref)

    @pl.when(pl.program_id(0) == 1)
    def _():
        project_rows(normed_ref, sib_ref, out_ref)


def project_rows(normed_ref, weight_ref, out_ref):
    weight = side_by_side(weight_ref)
    for start in range(0, normed_ref.shape[0], ROWS):
        part = pl.ds(start, ROWS)
        out_ref[0, part, :] = jnp.dot(
            normed_ref[part, :], weight, preferred_element_type=jnp.float32
        ).astype(jnp.bfloat16)


def in_spec(layer, width, cols, order):
    return pl.BlockSpec((1, 3, width, cols // 3), lambda *a: (layer, 0, 0, a[-1][order(*a[:-1])]))


def project(spots, layer, x, shift, scale, weight):
    rows, width = x.shape
    cols = 3 * weight.shape[3] // 2
    return call(
        project_kernel,
        "project",
        (2,),
        [
            once_block(rows, width),
            full_block(1, width),
            full_block(1, width),
            in_spec(layer, width, cols, lambda q: q),
        ],
        (
            full_block(width, rows),
            full_block(rows, width),
            pl.BlockSpec((1, rows, cols), lambda q, s: (q, 0, 0)),
        ),
        (
            jax.ShapeDtypeStruct((width, rows), jnp.bfloat16),
            jax.ShapeDtypeStruct((rows, width), jnp.bfloat16),
            jax.ShapeDtypeStruct((2, rows, cols), jnp.bfloat16),
        ),
        4 * rows * width * cols,
    )(spots, x, shift, scale, weight)


def project_more(spots, normed, mine, sib):
    rows, width = normed.shape
    size = mine.shape[2]
    return call(
        project_more_kernel,
        "project_more",
        (2,),
        [once_block(rows, width), full_block(1, 3, width, size), full_block(1, 3, width, size)],
        pl.BlockSpec((1, rows, 3 * size), lambda q, s: (q, 0, 0)),
        jax.ShapeDtypeStruct((2, rows, 3 * size), jnp.bfloat16),
        12 * rows * width * size,
    )(spots, normed, mine[None], sib[None])


def window_heads(proj_ref, ublk_ref, place, extra_ref=None):
    count = place.shape[0]
    heads = ublk_ref.shape[0]
    wide = heads * HEAD
    lane = lax.broadcasted_iota(jnp.int32, (count, 128), 1)
    items = []
    for window in range(proj_ref.shape[1] // count):
        rows = pl.ds(window * count, count)
        for pair in range(heads // 2):
            cols = pl.ds(pair * 128, 128)
            query, key, value = (
                proj_ref[0, rows, part * wide + pair * 128 : part * wide + pair * 128 + 128]
                for part in range(3)
            )
            kk = jnp.concatenate([key, place], axis=1)
            for half in range(2):
                mine = (lane < HEAD) if half == 0 else (lane >= HEAD)
                scaled = jnp.where(mine, query * HEAD**-0.5, 0.0).astype(jnp.bfloat16)
                above = None
                if extra_ref is not None:
                    above = jnp.where(mine, extra_ref[rows, cols], 0.0).astype(jnp.bfloat16)
                items.append((rows, pair, 2 * pair + half, kk, key, value, scaled, above))
    return items, lane


def head_scores(item, ublk_ref):
    query = jnp.concatenate([item[6], ublk_ref[item[2]]], axis=1)
    return lax.dot_general(item[3], query, CONTRACT_LAST, preferred_element_type=jnp.float32)


def head_probs(scores):
    expo = jnp.exp(scores - jnp.max(scores, axis=0, keepdims=True))
    return expo * (1.0 / jnp.sum(expo, axis=0, keepdims=True))


def ahead(items, first, middle, last):
    ready, count = first(items[0]), len(items)
    held = None
    for i in range(count):
        later = first(items[i + 1]) if i + 1 < count else None
        now = middle(ready)
        if i > 0:
            last(i - 1, held)
        ready, held = later, now
    last(count - 1, held)


def attend_kernel(_, proj_ref, ublk_ref, place_ref, out_ref):
    items, lane = window_heads(proj_ref, ublk_ref, place_ref[...])
    done = []

    def mix(i, probs):
        rows, pair, value = items[i][0], items[i][1], items[i][5]
        done.append(
            lax.dot_general(probs, value, CONTRACT_FIRST, preferred_element_type=jnp.float32)
        )
        if i % 2:
            out_ref[rows, pair * 128 : pair * 128 + 128] = jnp.where(
                lane < HEAD, done[i - 1], done[i]
            ).astype(jnp.bfloat16)

    ahead(
        items,
        lambda item: head_scores(item, ublk_ref),
        lambda scores: head_probs(scores).astype(jnp.bfloat16),
        mix,
    )


def attend(spots, first, proj, ublk, place):
    quarters, rows, cols = proj.shape
    count = place.shape[0]
    heads = ublk.shape[0] // 4
    pairs = rows * count * heads * quarters
    return call(
        attend_kernel,
        "attend",
        (quarters,),
        [
            pl.BlockSpec((1, rows, cols), lambda q, s: (q, 0, 0)),
            pl.BlockSpec((heads, count, 128), lambda q, s: (first + s[q], 0, 0)),
            full_block(count, 128),
        ],
        pl.BlockSpec((rows, heads * HEAD), lambda q, s: (0, q)),
        jax.ShapeDtypeStruct((rows, quarters * heads * HEAD), jnp.bfloat16),
        pairs * 768,
        pairs,
    )(spots, proj, ublk, place)


def join_kernel(
    _, own_ref, far_ref, w0_ref, w1_ref, w2_ref, w3_ref, x_ref, gate_ref, shift_ref, scale_ref,
    branch_ref, middle_ref, normed_ref, turned_ref,
):
    weights = [w0_ref[0], w1_ref[0], w2_ref[...], w3_ref[...]]
    branch = jnp.dot(
        jnp.concatenate([own_ref[...], far_ref[...]], axis=1),
        jnp.concatenate(weights, axis=0),
        preferred_element_type=jnp.float32,
    )
    branch_ref[...] = branch
    middle = x_ref[...] + gate_ref[...] * branch
    middle_ref[...] = middle
    unit, _ = row_norm(middle)
    normed = (unit * (1.0 + scale_ref[...]) + shift_ref[...]).astype(jnp.bfloat16)
    normed_ref[...] = normed
    turned_ref[...] = normed.T


def row_tile(cols):
    return pl.BlockSpec((ROWS, cols), lambda i, s: (i, 0))


def quarter_rows(layer, r, size, width):
    return pl.BlockSpec(
        (1, size, width), lambda i, s: (layer, s[r], 0), pipeline_mode=pl.Buffered(1)
    )


def join(spots, layer, own, far, weight, recv, sib, x, gate, shift, scale):
    rows, width = x.shape
    half = own.shape[1]
    tile = row_tile(width)
    size = half // 2
    return call(
        join_kernel,
        "join",
        (rows // ROWS,),
        [
            row_tile(half),
            row_tile(half),
            quarter_rows(layer, 0, size, width),
            quarter_rows(layer, 1, size, width),
            once_block(size, width),
            once_block(size, width),
            tile,
        ]
        + [full_block(1, width)] * 3,
        (tile, tile, tile, pl.BlockSpec((width, ROWS), lambda i, s: (0, i))),
        (
            jax.ShapeDtypeStruct((rows, width), jnp.float32),
            jax.ShapeDtypeStruct((rows, width), jnp.float32),
            jax.ShapeDtypeStruct((rows, width), jnp.bfloat16),
            jax.ShapeDtypeStruct((width, rows), jnp.bfloat16),
        ),
        2 * rows * width * width,
    )(spots, own, far, weight, weight, recv, sib, x, gate, shift, scale)


SLOPE = float(np.sqrt(2 / np.pi))


def up_kernel(_, normed_ref, weight_ref, bias_ref, pre_ref, hidden_ref):
    starts = list(range(0, normed_ref.shape[0], ROWS))

    def product(start):
        return (
            jnp.dot(
                normed_ref[pl.ds(start, ROWS), :], weight_ref[0], preferred_element_type=jnp.float32
            )
            + bias_ref[0, 0]
        )

    pre = product(starts[0])
    for start, following in zip(starts, starts[1:] + [None]):
        later = None if following is None else product(following)
        part = pl.ds(start, ROWS)
        pre_ref[0, part, :] = pre
        bent = jnp.tanh(pre * (SLOPE + (SLOPE * 0.044715) * (pre * pre)))
        half = 0.5 * pre
        hidden_ref[0, part, :] = (half + half * bent).astype(jnp.bfloat16)
        pre = later


def up_spec(layer, own, width, cols, step, order):
    if own:
        per = cols // step
        return pl.BlockSpec(
            (1, width, step), lambda *a: (layer, 0, a[-1][order(*a[:-1])[0]] * per + order(*a[:-1])[1])
        )
    return pl.BlockSpec((1, width, step), lambda *a: (0, 0, order(*a[:-1])[1]))


def up(spots, layer, quarter, normed, weight, bias):
    rows, width = normed.shape
    cols = bias.shape[3]
    step = cols // 2
    own = quarter is None
    count = 2 if own else 1
    tile = pl.BlockSpec((1, rows, step), lambda q, j, s: (q, 0, j))
    return call(
        up_kernel,
        "up",
        (count, cols // step),
        [
            once_block(rows, width),
            up_spec(layer, own, width, cols, step, lambda q, j: (q, j)),
            pl.BlockSpec((1, 1, 1, step), lambda q, j, s: (layer, s[q if own else quarter], 0, j)),
        ],
        (tile, tile),
        (
            jax.ShapeDtypeStruct((count, rows, cols), jnp.float32),
            jax.ShapeDtypeStruct((count, rows, cols), jnp.bfloat16),
        ),
        2 * count * rows * width * cols,
        count * rows * cols,
    )(spots, normed, weight if own else weight[None], bias)


def down_kernel(
    _, own_ref, far_ref, sib_ref, w0_ref, w1_ref, w2_ref, w3_ref, middle_ref, gate_ref, branch_ref, out_ref
):
    total = jnp.dot(own_ref[0], w0_ref[0], preferred_element_type=jnp.float32)
    total += jnp.dot(own_ref[1], w1_ref[0], preferred_element_type=jnp.float32)
    total += jnp.dot(far_ref[0], w2_ref[...], preferred_element_type=jnp.float32)
    total += jnp.dot(sib_ref[0], w3_ref[...], preferred_element_type=jnp.float32)
    branch_ref[...] = total
    out_ref[...] = middle_ref[...] + gate_ref[...] * total


def down(spots, layer, own, far, far_sib, weight, recv, sib, middle, gate):
    rows, width = middle.shape
    cols = own.shape[2]
    tile = row_tile(width)
    hidden, single = (pl.BlockSpec((n, ROWS, cols), lambda i, s: (0, i, 0)) for n in (2, 1))
    return call(
        down_kernel,
        "down",
        (rows // ROWS,),
        [
            hidden,
            single,
            single,
            quarter_rows(layer, 0, cols, width),
            quarter_rows(layer, 1, cols, width),
            once_block(cols, width),
            once_block(cols, width),
            tile,
            full_block(1, width),
        ],
        (tile, tile),
        (
            jax.ShapeDtypeStruct((rows, width), jnp.float32),
            jax.ShapeDtypeStruct((rows, width), jnp.float32),
        ),
        8 * rows * width * cols,
    )(spots, own, far, far_sib, weight, weight, recv, sib, middle, gate)


def feed_back_kernel(
    _, gdb_ref, hidden_ref, pre_ref, turned_ref, down_ref, up_ref,
    down_grad_ref, up_grad_ref, bias_grad_ref, normed_grad_ref, gpre_ref, total_ref,
):
    starts = list(range(0, gdb_ref.shape[0], ROWS))
    columns = gdb_ref.shape[1] // 4
    sums = jnp.zeros(bias_grad_ref.shape, jnp.float32)

    def product(start):
        return lax.dot_general(
            gdb_ref[pl.ds(start, ROWS), :], down_ref[0], CONTRACT_LAST, preferred_element_type=jnp.float32
        )

    grad_hidden = product(starts[0])
    for i, start in enumerate(starts):
        later = product(starts[i + 1]) if i + 1 < len(starts) else None
        if i < 4:
            part = pl.ds(i * columns, columns)
            down_grad_ref[:, part] = lax.dot_general(
                hidden_ref[0], gdb_ref[:, part], CONTRACT_FIRST, preferred_element_type=jnp.float32
            ).astype(jnp.bfloat16)
        part = pl.ds(start, ROWS)
        pre = pre_ref[0, part, :]
        square = pre * pre
        bent = jnp.tanh(pre * (SLOPE + (SLOPE * 0.044715) * square))
        half = 0.5 + 0.5 * bent
        slope = half + (pre * (half * (1.0 - bent))) * (SLOPE + (3 * 0.044715 * SLOPE) * square)
        grad_pre = (grad_hidden * slope).astype(jnp.bfloat16)
        gpre_ref[part, :] = grad_pre
        sums += jnp.sum(grad_pre.astype(jnp.float32), axis=0, keepdims=True)
        grad_hidden = later
    bias_grad_ref[...] = sums
    up_grad_ref[...] = jnp.dot(
        turned_ref[...], gpre_ref[...], preferred_element_type=jnp.float32
    ).astype(jnp.bfloat16)

    def each(store):
        for start in starts:
            part = pl.ds(start, ROWS)
            term = lax.dot_general(
                gpre_ref[part, :], up_ref[0], CONTRACT_LAST, preferred_element_type=jnp.float32
            )
            store(part, term)

    step, steps = pl.program_id(0), pl.num_programs(0)

    @pl.when(step == 0)
    def _():
        def store(part, term):
            total_ref[part, :] = term

        each(store)

    @pl.when(step == steps - 1)
    def _():
        def store(part, term):
            normed_grad_ref[part, :] = (total_ref[part, :] + term).astype(jnp.bfloat16)

        each(store)


def feed_back(spots, layer, own, r, gdb, hidden, pre, turned, down_weight, up_weight):
    rows, width = gdb.shape
    cols = hidden.shape[2]
    step = cols // 2
    per = cols // step
    if own:
        down_spec = pl.BlockSpec((1, step, width), lambda j, s: (layer, s[r] * per + j, 0))
    else:
        down_weight, up_weight = down_weight[None], up_weight[None]
        down_spec = pl.BlockSpec((1, step, width), lambda j, s: (0, j, 0))
    return call(
        feed_back_kernel,
        "feed_back",
        (per,),
        [
            once_block(rows, width),
            pl.BlockSpec((1, rows, step), lambda j, s: (r if own else 0, 0, j)),
            pl.BlockSpec((1, rows, step), lambda j, s: (r if own else 0, 0, j)),
            once_block(width, rows),
            down_spec,
            up_spec(layer, own, width, cols, step, lambda j: (r, j)),
        ],
        (
            pl.BlockSpec((step, width), lambda j, s: (j, 0)),
            pl.BlockSpec((width, step), lambda j, s: (0, j)),
            pl.BlockSpec((1, step), lambda j, s: (0, j)),
            full_block(rows, width),
        ),
        (
            jax.ShapeDtypeStruct((cols, width), jnp.bfloat16),
            jax.ShapeDtypeStruct((width, cols), jnp.bfloat16),
            jax.ShapeDtypeStruct((1, cols), jnp.float32),
            jax.ShapeDtypeStruct((rows, width), jnp.bfloat16),
        ),
        8 * rows * width * cols,
        rows * cols,
        scratch=[pltpu.VMEM((rows, step), jnp.bfloat16), pltpu.VMEM((rows, width), jnp.float32)],
    )(spots, gdb, hidden, pre, turned, down_weight, up_weight)


def join_back_kernel(
    _, one_ref, two_ref, three_ref, four_ref, g_ref, middle_ref, branch_ref, own_ref, far_ref,
    w0_ref, w1_ref, w2_ref, w3_ref, gate_ref, scale_ref,
    grad_middle_ref, grad_own_ref, grad_far_ref, own_grad_ref, far_grad_ref, sums_ref, total_ref,
):
    one, two, three, four = (
        ref[...].astype(jnp.float32) for ref in (one_ref, two_ref, three_ref, four_ref)
    )
    partial = (one + two) + (three + four)
    pulled, shift_sum, scale_sum = norm_back(middle_ref[...], partial, scale_ref[...])
    grad_middle = g_ref[...] + pulled
    grad_middle_ref[...] = grad_middle
    gate_sum = jnp.sum(grad_middle * branch_ref[...], axis=0, keepdims=True)
    grad_branch = (gate_ref[...] * grad_middle).astype(jnp.bfloat16)
    weights = jnp.concatenate([w0_ref[0], w1_ref[0], w2_ref[...], w3_ref[...]], axis=0)
    grad_att = lax.dot_general(
        grad_branch, weights, CONTRACT_LAST, preferred_element_type=jnp.float32
    ).astype(jnp.bfloat16)
    half = own_ref.shape[1]
    grad_own_ref[...] = grad_att[:, :half]
    grad_far_ref[...] = grad_att[:, half:]
    att = jnp.concatenate([own_ref[...], far_ref[...]], axis=1)
    weight_term = lax.dot_general(
        att, grad_branch, CONTRACT_FIRST, preferred_element_type=jnp.float32
    )
    sums = jnp.concatenate([shift_sum, scale_sum, gate_sum], axis=0)
    step = pl.program_id(0)

    @pl.when(step == 0)
    def _():
        total_ref[...] = weight_term
        sums_ref[...] = sums

    @pl.when(step > 0)
    def _():
        total_ref[...] += weight_term
        sums_ref[...] += sums

    @pl.when(step == pl.num_programs(0) - 1)
    def _():
        own_grad_ref[...] = total_ref[:half, :].astype(jnp.bfloat16)
        far_grad_ref[...] = total_ref[half:, :].astype(jnp.bfloat16)


def join_back(spots, layer, partials, g, middle, branch, own, far, weight, recv, sib, gate, scale):
    rows, width = g.shape
    half = own.shape[1]
    size = half // 2
    tile = row_tile(width)
    return call(
        join_back_kernel,
        "join_back",
        (rows // ROWS,),
        [tile] * 7
        + [
            row_tile(half),
            row_tile(half),
            quarter_rows(layer, 0, size, width),
            quarter_rows(layer, 1, size, width),
            once_block(size, width),
            once_block(size, width),
        ]
        + [full_block(1, width)] * 2,
        (
            tile,
            row_tile(half),
            row_tile(half),
            full_block(half, width),
            full_block(half, width),
            full_block(3, width),
        ),
        (
            jax.ShapeDtypeStruct((rows, width), jnp.float32),
            jax.ShapeDtypeStruct((rows, half), jnp.bfloat16),
            jax.ShapeDtypeStruct((rows, half), jnp.bfloat16),
            jax.ShapeDtypeStruct((half, width), jnp.bfloat16),
            jax.ShapeDtypeStruct((half, width), jnp.bfloat16),
            jax.ShapeDtypeStruct((3, width), jnp.float32),
        ),
        4 * rows * width * width,
        scratch=[pltpu.VMEM((width, width), jnp.float32)],
    )(spots, *partials, g, middle, branch, own, far, weight, weight, recv, sib, gate, scale)


def attend_back_kernel(_, proj_ref, grad_ref, ublk_ref, place_ref, out_ref, table_ref):
    place = place_ref[...]
    items, lane = window_heads(proj_ref, ublk_ref, place, grad_ref)
    wide = ublk_ref.shape[0] * HEAD
    tables = {}
    done = []

    def first(item):
        grad_probs = lax.dot_general(
            item[5], item[7], CONTRACT_LAST, preferred_element_type=jnp.float32
        )
        return head_scores(item, ublk_ref), grad_probs

    def middle(pair):
        probs, grad_probs = head_probs(pair[0]), pair[1]
        inner = jnp.sum(probs * grad_probs, axis=0, keepdims=True)
        return probs.astype(jnp.bfloat16), (probs * (grad_probs - inner)).astype(jnp.bfloat16)

    def last(i, held):
        probs, grad_scores = held
        rows, pair, head, _, key, _, scaled, above = items[i]
        both = jnp.dot(
            grad_scores, jnp.concatenate([scaled, place], axis=1), preferred_element_type=jnp.float32
        )
        grad_value = jnp.dot(probs, above, preferred_element_type=jnp.float32)
        grad_query = lax.dot_general(
            grad_scores,
            (key * HEAD**-0.5).astype(jnp.bfloat16),
            CONTRACT_FIRST,
            preferred_element_type=jnp.float32,
        )
        tables[head] = both[:, 128:] if head not in tables else tables[head] + both[:, 128:]
        done.append((grad_query, both[:, :128], grad_value))
        if i % 2:
            (q0, k0, v0), (q1, k1, v1) = done[i - 1], done[i]
            for part, value in enumerate((jnp.where(lane < HEAD, q0, q1), k0 + k1, v0 + v1)):
                out_ref[0, rows, part * wide + pair * 128 : part * wide + pair * 128 + 128] = (
                    value.astype(jnp.bfloat16)
                )

    ahead(items, first, middle, last)
    for head, value in tables.items():
        table_ref[head] = value


def attend_back(spots, first, proj, grad, ublk, place):
    quarters, rows, cols = proj.shape
    count = place.shape[0]
    heads = ublk.shape[0] // 4
    pairs = rows * count * heads * quarters
    return call(
        attend_back_kernel,
        "attend_back",
        (quarters,),
        [
            pl.BlockSpec((1, rows, cols), lambda q, s: (q, 0, 0)),
            pl.BlockSpec((rows, heads * HEAD), lambda q, s: (0, q)),
            pl.BlockSpec((heads, count, 128), lambda q, s: (first + s[q], 0, 0)),
            full_block(count, 128),
        ],
        (
            pl.BlockSpec((1, rows, cols), lambda q, s: (q, 0, 0)),
            pl.BlockSpec((heads, count, 128), lambda q, s: (s[q], 0, 0)),
        ),
        (
            jax.ShapeDtypeStruct(proj.shape, jnp.bfloat16),
            jax.ShapeDtypeStruct((ublk.shape[0] // 2, count, 128), jnp.float32),
        ),
        pairs * 1536,
        pairs,
    )(spots, proj, grad, ublk, place)


def in_grad_kernel(_, turned_ref, grad_ref, mine_ref, sib_ref):
    def store(ref):
        for part in range(3):
            size = ref.shape[2]
            ref[part] = jnp.dot(
                turned_ref[...],
                grad_ref[0, :, part * size : part * size + size],
                preferred_element_type=jnp.float32,
            ).astype(jnp.bfloat16)

    @pl.when(pl.program_id(0) == 0)
    def _():
        store(sib_ref)

    @pl.when(pl.program_id(0) == 1)
    def _():
        store(mine_ref)


def in_grad(spots, turned, grad):
    width, rows = turned.shape
    cols = grad.shape[2]
    size = cols // 3
    out = jax.ShapeDtypeStruct((3, width, size), jnp.bfloat16)
    return call(
        in_grad_kernel,
        "in_grad",
        (2, 2),
        [
            pl.BlockSpec((width // 2, rows), lambda q, j, s: (j, 0)),
            pl.BlockSpec((1, rows, cols), lambda q, j, s: (1 - q, 0, 0)),
        ],
        (
            pl.BlockSpec((3, width // 2, size), lambda q, j, s: (0, q * j, 0)),
            pl.BlockSpec((3, width // 2, size), lambda q, j, s: (0, jnp.maximum(q, j), 0)),
        ),
        (out, out),
        4 * rows * width * cols,
    )(spots, turned, grad)


def project_back_kernel(
    _, own_ref, far_ref, w0_ref, w1_ref, w2_ref, w3_ref, x_ref, middle_ref, scale_ref, out_ref, sums_ref
):
    total = None
    for grad, weight in (
        (own_ref[0], w0_ref), (own_ref[1], w1_ref), (far_ref[0], w2_ref), (far_ref[1], w3_ref)
    ):
        term = lax.dot_general(
            grad, side_by_side(weight), CONTRACT_LAST, preferred_element_type=jnp.float32
        )
        total = term if total is None else total + term
    pulled, shift_sum, scale_sum = norm_back(x_ref[...], total, scale_ref[...])
    out_ref[...] = middle_ref[...] + pulled
    sums = jnp.concatenate([shift_sum, scale_sum], axis=0)

    @pl.when(pl.program_id(0) == 0)
    def _():
        sums_ref[...] = sums

    @pl.when(pl.program_id(0) > 0)
    def _():
        sums_ref[...] += sums


def project_back(spots, layer, own, far, weight, mine, sib, x, grad_middle, scale):
    rows, width = x.shape
    cols = own.shape[2]
    tile = row_tile(width)
    grad = pl.BlockSpec((2, ROWS, cols), lambda i, s: (0, i, 0))

    return call(
        project_back_kernel,
        "project_back",
        (rows // ROWS,),
        [grad, grad]
        + [in_spec(layer, width, cols, lambda i, r=r: r) for r in (0, 1)]
        + [full_block(1, 3, width, cols // 3)] * 2
        + [tile, tile, full_block(1, width)],
        (tile, full_block(2, width)),
        (
            jax.ShapeDtypeStruct((rows, width), jnp.float32),
            jax.ShapeDtypeStruct((2, width), jnp.float32),
        ),
        8 * rows * width * cols,
    )(spots, own, far, weight, weight, mine[None], sib[None], x, grad_middle, scale)


def modulation_kernel(_, activated_ref, rows_ref, out_ref):
    out_ref[0, 0] = lax.dot_general(
        activated_ref[...], rows_ref[0, 0], CONTRACT_FIRST, preferred_element_type=jnp.float32
    )


def modulation_back(spots, activated, rows):
    layers, kinds, _, cols = rows.shape
    count, width = activated.shape
    values = jnp.concatenate(split_bits(rows), axis=2)
    return call(
        modulation_kernel,
        "modulation_back",
        (layers, kinds),
        [
            full_block(3 * count, width),
            pl.BlockSpec((1, 1, 3 * count, cols), lambda l, k, s: (l, k, 0, 0)),
        ],
        pl.BlockSpec((1, 1, width, cols), lambda l, k, s: (l, k, 0, 0)),
        jax.ShapeDtypeStruct((layers, kinds, width, cols), jnp.float32),
        6 * layers * kinds * count * width * cols,
    )(spots, jnp.concatenate([activated.astype(jnp.bfloat16)] * 3), values)


SWAP = [(0, 1), (1, 0)]


def either(flag, one, two):
    return jnp.where(flag, one, two)


def split_bits(values):
    parts = []
    for _ in range(3):
        part = lax.reduce_precision(values, 8, 7)
        parts.append(part.astype(jnp.bfloat16))
        values = values - part
    return parts


def place_maps(layer, frames):
    extents = window_shape(layer)
    count = extents[0] * extents[1] * extents[2]
    place = np.arange(count)
    positions = (place // (extents[1] * extents[2]), place // extents[2] % extents[1], place % extents[2])
    hots = []
    width = sum(e for e in extents if e > 1)
    levels = sum(2 * e - 1 for e in extents if e > 1)
    pick = np.zeros((levels, width, width), np.float32)
    column = base = 0
    for position, extent in zip(positions, extents):
        if extent == 1:
            continue
        spots = jnp.asarray(position, jnp.int32)
        if extent == FRAMES and layer == 1:
            spots = frames[spots]
        hots.append((spots[:, None] == jnp.arange(extent, dtype=jnp.int32)[None, :]).astype(jnp.float32))
        for i in range(extent):
            for j in range(extent):
                pick[base + i - j + extent - 1, column + i, column + j] = 1
        column += extent
        base += 2 * extent - 1
    return jnp.concatenate(hots, axis=1), pick


def bias_blocks(table, hot, pick):
    pairs = jnp.einsum("hx,xij->hij", table, pick, precision=HIGH)
    spread = jnp.einsum("ai,hij->haj", hot, pairs, precision=HIGH)
    parts = split_bits(spread)
    room = 128 - 3 * hot.shape[1]
    padded = jnp.concatenate(parts + [jnp.zeros(spread.shape[:2] + (room,), jnp.bfloat16)], axis=2)
    one = hot.astype(jnp.bfloat16)
    place = jnp.concatenate([one] * 3 + [jnp.zeros((hot.shape[0], room), jnp.bfloat16)], axis=1)
    return padded, place


def table_grad(acc, hot, pick):
    width = hot.shape[1]
    pairs = jnp.einsum("hbi,bj->hij", acc[:, :, :width], hot, precision=HIGH)
    return jnp.einsum("hij,xij->hx", pairs, pick, precision=HIGH)


def per_device_pair(
    tokens,
    cotangent,
    group_start,
    band_index,
    class_label,
    time_table,
    class_table,
    modulation_weight,
    modulation_bias,
    input_weight,
    output_weight,
    space_offsets,
    time_offsets,
    up_weight,
    up_bias,
    down_weight,
):
    core = lax.axis_index("core")
    chip_axes = ("z", "y")
    chip = lax.axis_index(chip_axes)
    side = lax.axis_index("mp")
    chips = lax.axis_size(chip_axes)
    low_side, first_core = side == 0, core == 0
    rows, width = tokens.shape
    half = width // 2
    bf16, f32 = jnp.bfloat16, jnp.float32
    spots = jnp.stack([core, 1 - core]).astype(jnp.int32)

    def swap_side(value):
        return lax.ppermute(value, "mp", SWAP)

    def swap_core(value):
        return lax.ppermute(value, "core", SWAP)

    def half_of(value, axis):
        size = value.shape[axis] // 2
        return lax.dynamic_slice_in_dim(value, core * size, size, axis)

    def after(value, *others):
        return lax.optimization_barrier((value,) + others)[0]

    def in_order(flag, one, two):
        return [either(flag, one, two), either(flag, two, one)]

    def gather_dp(value):
        stack = value[None]
        stack = jnp.concatenate(in_order(first_core, stack, swap_core(stack)))
        distance = 1
        while distance < chips:
            got = lax.ppermute(stack, chip_axes, [(i, i ^ distance) for i in range(chips)])
            stack = jnp.concatenate(in_order((chip // distance) % 2 == 0, stack, got))
            distance *= 2
        return stack

    here_y, here_z = lax.axis_index("y"), lax.axis_index("z")
    size_z = lax.axis_size("z")

    def swap_y(value):
        return lax.ppermute(value, "y", SWAP)

    def eighth(value, axis):
        size = value.shape[axis] // 4
        return lax.dynamic_slice_in_dim(value, (2 * core + here_y) * size, size, axis)

    def quarter(got, axis, start=None, use=None):
        got = got if start is None else after(got, start)
        other = swap_y(got)
        other = other if use is None else after(other, use)
        return jnp.concatenate(in_order(here_y == 0, got, other), axis=axis)

    in_weight = input_weight.transpose(0, 2, 1, 3)
    first_piece = eighth(in_weight[0], 2)
    marked = after(jnp.where(group_start > 0, band_index, -1), first_piece)
    every = lax.all_gather(marked, chip_axes + ("core",), tiled=True)
    mine = lax.axis_index(chip_axes + ("core",))
    order = jnp.arange(every.shape[0], dtype=jnp.int32)
    latest = jnp.max(jnp.where((every >= 0) & (order <= mine), order, -1))
    current = jnp.sum(jnp.where(order == latest, every, 0)) + jnp.where(latest < 0, -1, 0)
    band_hot = (current == jnp.arange(time_table.shape[0], dtype=jnp.int32)).astype(f32)
    class_hot = (class_label[0] == jnp.arange(class_table.shape[0], dtype=jnp.int32)).astype(f32)
    condition = jnp.sum(band_hot[:, None] * time_table, axis=0) + jnp.sum(
        class_hot[:, None] * class_table, axis=0
    )
    activated = jax.nn.silu(condition).astype(bf16)
    local_modulation = (
        jnp.einsum("d,ldcf->lcf", activated, modulation_weight, preferred_element_type=f32)
        + modulation_bias
    )
    modulation_got = swap_side(local_modulation)
    modulation = jnp.concatenate(in_order(low_side, local_modulation, modulation_got), axis=2)

    far_in, far_up, far_down = ([None, None] for _ in range(3))
    far_small = swap_side(
        jnp.concatenate([space_offsets.reshape(-1), time_offsets.reshape(-1), up_bias.reshape(-1)])
    )
    cut_one = space_offsets.size
    cut_two = cut_one + time_offsets.size
    tables = (
        jnp.concatenate([space_offsets, far_small[:cut_one].reshape(space_offsets.shape)]),
        jnp.concatenate([time_offsets, far_small[cut_one:cut_two].reshape(time_offsets.shape)]),
    )
    biases = (up_bias.reshape(2, 2, 1, -1), far_small[cut_two:].reshape(2, 2, 1, -1))

    def after_all(values, *others):
        return lax.optimization_barrier((values,) + others)[0]

    def fetch(layer, trigger):
        sources = after_all((in_weight, up_weight, down_weight), trigger)
        return [
            swap_side(eighth(source[layer], axis)) for source, axis in zip(sources, (2, 1, 0))
        ]

    fetched = [fetch(0, modulation_got), None]
    fetched[0][0] = swap_side(first_piece)
    out_got = swap_side(eighth(after(output_weight, modulation_got), 1))
    far_out, far_in, far_up, far_down = ([None, None] for _ in range(4))

    split = lax.dynamic_slice_in_dim(tokens, (1 - side) * (rows - ROWS), ROWS, 0).reshape(8, 2, 16, width)
    kept = lax.dynamic_index_in_dim(split, side, 1, keepdims=False)
    got = swap_side(lax.dynamic_index_in_dim(split, 1 - side, 1, keepdims=False))
    shared = jnp.concatenate(in_order(low_side, kept, got), axis=0)
    whole = lax.dynamic_slice_in_dim(tokens, side * ROWS, rows - ROWS, 0)
    whole = whole.reshape(2, 16, 2, 16, width).transpose(0, 2, 1, 3, 4)
    x = jnp.concatenate([whole.reshape(-1, width), shared.reshape(-1, width)], axis=0).astype(f32)

    frames = jnp.where(
        low_side,
        jnp.asarray([0, 1, 2, 3, 4], jnp.int32),
        jnp.asarray([3, 4, 2, 0, 1], jnp.int32),
    )
    maps = [place_maps(layer, frames) for layer in range(2)]

    def send_cotangent(value):
        chunks = value.reshape(5, ROWS, width)
        return chunks, swap_side(jnp.stack([chunks[1], chunks[3]]))

    def turn_cotangent(chunks, got):
        kept = [
            either(low_side, chunks[0], chunks[2]),
            either(low_side, chunks[2], chunks[4]),
            either(low_side, chunks[4], chunks[0]),
        ]
        ordered = jnp.concatenate([jnp.stack(kept), got]).reshape(5, 8, 4, 8, width)
        return ordered.transpose(2, 0, 1, 3, 4).reshape(rows, width).astype(f32)

    saved = []
    for layer in range(2):
        shift_one, scale_one, gate_one, shift_two, scale_two, gate_two = [
            modulation[layer, number][None] for number in range(6)
        ]
        ublk, place = bias_blocks(tables[layer], *maps[layer])
        turned, normed, own_proj = project(
            spots, layer, x, after(shift_one, far_small, fetched[layer][0]), scale_one, in_weight
        )
        if layer == 0:
            fetched[1] = fetch(1, own_proj)
            out_quarters = quarter(out_got, 1, own_proj)
            far_in[0] = [quarter(fetched[0][0], 2)]
        else:
            far_in[1] = [quarter(fetched[1][0], 2, first_hidden, x)]
        own_att = attend(spots, 0, after(own_proj, far_in[layer][0]), ublk, place)
        far_in[layer].append(swap_core(far_in[layer][0]))
        far_proj = project_more(spots, after(normed, own_att), *far_in[layer])
        far_out[layer] = [out_quarters[layer], swap_core(after(out_quarters, own_att)[layer])]
        far_att = attend(spots, 2, far_proj, ublk, place)
        branch, middle, normed_two, turned_two = join(
            spots, layer, own_att, far_att, output_weight, *far_out[layer], x, gate_one, shift_two, scale_two
        )
        start, use = (far_proj, normed_two) if layer == 0 else (first_hidden, own_proj)
        far_up[layer] = [quarter(fetched[layer][1], 1, start, use)]
        far_down[layer] = [quarter(fetched[layer][2], 0, start, use)]
        for kept in (far_up, far_down):
            kept[layer].append(swap_core(kept[layer][0]))
        if layer == 1:
            chunks, cotangent_got = send_cotangent(after(cotangent, far_att))
        own_pre, own_hidden = up(spots, layer, None, normed_two, up_weight, biases[0])
        far_pre, far_hidden = [None, None], [None, None]
        for r in range(2):
            ready = after(normed_two, far_hidden[0], *fetched[1]) if layer == 0 and r == 1 else normed_two
            far_pre[r], far_hidden[r] = up(spots, layer, r, ready, far_up[layer][r], biases[1])
        first_hidden = far_hidden[1]
        if layer == 1:
            g = turn_cotangent(chunks, after(cotangent_got, far_hidden[1]))
        branch_two, out = down(
            spots, layer, own_hidden, *far_hidden, down_weight, *far_down[layer],
            middle if layer == 0 else after(middle, g), gate_two,
        )
        saved.append(
            (
                x, turned, own_proj, far_proj, own_att, far_att, branch, middle, turned_two,
                own_pre, own_hidden, far_pre, far_hidden, branch_two, ublk, place,
            )
        )
        if layer == 0:
            parts = out.reshape(5, 2, 128, width)
            kept = lax.dynamic_index_in_dim(parts, side, 1, keepdims=False)
            sent = lax.dynamic_index_in_dim(parts, 1 - side, 1, keepdims=False).astype(bf16)
            got = swap_side(sent).astype(f32)
            shared = jnp.stack(in_order(low_side, kept[4], got[4]))
            x = jnp.concatenate([kept[:4], shared, got[:4]])
            x = x.reshape(5, 2, 8, 2, 8, width).transpose(1, 3, 0, 2, 4, 5).reshape(rows, width)

    parts = out.reshape(2, 2, 5, 8, 8, width).transpose(2, 0, 3, 1, 4, 5).reshape(5, 2, 8, 16, width)
    result_sent = parts[3:].astype(bf16)
    result_got = swap_side(result_sent)
    got = result_got.astype(f32)
    pair = jnp.stack(in_order(low_side, parts[:2], got), axis=2)
    pair = pair.reshape(2, 2, 16, 16, width).transpose(0, 2, 1, 3, 4).reshape(-1, width)
    shared = parts[2].transpose(1, 0, 2, 3).reshape(-1, width)
    result = either(
        low_side, jnp.concatenate([pair, shared], axis=0), jnp.concatenate([shared, pair], axis=0)
    )

    def crossing(mine, sib):
        return (mine.astype(f32) + swap_core(sib).astype(f32)).astype(bf16)

    def joined(mine, sib, got):
        return (mine.astype(f32) + swap_core(sib).astype(f32) + got.astype(f32)).astype(bf16)

    def turn_z(value, distance):
        return lax.ppermute(value, "z", [(i, (i + distance) % size_z) for i in range(size_z)])

    def y_sent(value):
        halves = value.reshape((2, -1) + value.shape[1:])
        kept = lax.dynamic_index_in_dim(halves, here_y, 0, keepdims=False)
        return kept, swap_y(lax.dynamic_index_in_dim(halves, 1 - here_y, 0, keepdims=False))

    def z_sent(kept, got):
        total = (kept.astype(f32) + got.astype(f32)).astype(bf16)
        parts = total.reshape((size_z, -1) + total.shape[1:])
        sent = [
            lax.dynamic_index_in_dim(parts, (here_z + k) % size_z, 0, keepdims=False)
            for k in range(size_z)
        ]
        return [sent[0]] + [turn_z(sent[k], k) for k in range(1, size_z)]

    def z_back(parts):
        total = sum(part.astype(f32) for part in parts).astype(bf16)
        return [total] + [turn_z(total, k) for k in range(1, size_z)]

    def y_back(parts):
        row = jnp.stack(parts[::-1] + parts[:0:-1])
        half = lax.dynamic_slice_in_dim(row, size_z - 1 - here_z, size_z, 0)
        half = half.reshape((-1,) + half.shape[2:])
        return half, swap_y(half)

    def both_quarters(half, got):
        full = jnp.concatenate(in_order(here_y == 0, half, got))
        other = jnp.concatenate(in_order(here_y == 0, swap_core(half), swap_core(got)))
        return in_order(first_core, full, other)

    def by_quarter(value):
        parts = value.reshape(2, -1, value.shape[-1])
        return parts[0], parts[1]

    collected, waiting, first_sums = [None, None], (result_sent,), ()
    sums = [{}, {}]
    steps = (y_sent, z_sent, z_back, y_back)

    def advance(trigger, *names):
        marks = []
        for name in names:
            value, step = sums[0][name]
            value = after_all(tuple(value), trigger)
            sums[0][name] = (steps[step](*value) if step < 2 else steps[step](value), step + 1)
            marks.append(sums[0][name][0][0])
        return marks

    def both_cores(value):
        return in_order(first_core, value, swap_core(value))

    for layer in (1, 0):
        shift_one, scale_one, gate_one, shift_two, scale_two, gate_two = [
            modulation[layer, number][None] for number in range(6)
        ]
        (
            x, turned, own_proj, far_proj, own_att, far_att, branch, middle, turned_two,
            own_pre, own_hidden, far_pre, far_hidden, branch_two, ublk, place,
        ) = saved[layer]
        gdb = (gate_two * g).astype(bf16)
        gate_two_grad = jnp.sum(g * branch_two, axis=0)

        def feed(own, r, *first):
            hidden, pre = (own_hidden, own_pre) if own else (far_hidden[r], far_pre[r])
            weights = (down_weight, up_weight) if own else (far_down[layer][r], far_up[layer][r])
            return feed_back(
                spots, layer, own, r, after(gdb, *first), hidden, pre, turned_two, *weights
            )

        far_sib = feed(False, 1, *waiting)
        far_mine = feed(False, 0, far_sib[0])
        far_down_sum, far_up_sum = crossing(far_mine[0], far_sib[0]), crossing(far_mine[1], far_sib[1])
        own_sib = feed(True, 1, far_down_sum, far_up_sum, *([result_got] if layer == 1 else []))
        down_got = swap_side(far_down_sum)
        own_mine = feed(True, 0, own_sib[0])
        far, own = (far_mine, far_sib), (own_mine, own_sib)
        grad_middle, grad_own, grad_far, own_out, far_out_grad, sums_two = join_back(
            spots, layer, [far[1][3], far[0][3], own[1][3], own[0][3]], g, middle, branch, own_att, far_att,
            output_weight, *far_out[layer], gate_one, scale_two,
        )
        down_sum = joined(own_mine[0], own_sib[0], down_got)
        up_got = swap_side(after(far_up_sum, down_got))

        far_grad, far_acc = attend_back(
            spots, 2, far_proj, after(grad_far, down_sum), ublk, place
        )
        in_mine, in_sib = in_grad(spots, turned, far_grad)
        own_grad, own_acc = attend_back(
            spots, 0, own_proj, after(grad_own, in_mine), ublk, place
        )
        far_in_sum = crossing(in_mine, in_sib)
        far_out_sum = crossing(*by_quarter(after(far_out_grad, in_mine)))
        up_sum = joined(own_mine[1], own_sib[1], up_got)
        in_mine, in_sib = in_grad(
            spots, after(turned, far_in_sum, far_out_sum, up_sum), own_grad
        )
        in_got, out_got = swap_side(far_in_sum), swap_side(far_out_sum)
        g, sums_one = project_back(
            spots, layer, own_grad, far_grad, in_weight, *far_in[layer], x,
            after(grad_middle, in_mine, *first_sums), scale_one,
        )
        out_sum = joined(*by_quarter(own_out), out_got)
        in_sum = joined(in_mine, in_sib, in_got)
        cut = in_sum.size // in_sum.shape[2]
        last = jnp.concatenate([part.reshape(-1, in_sum.shape[2]) for part in (in_sum, out_sum)])
        sums[layer]["last"] = ((last,), 0)
        if layer == 0:
            sums_one, g = after_all((sums_one, g), *advance(g, "last"))
            second_sums = lax.psum(after_all((down_sum, up_sum), *first_sums), chip_axes)
        table_rows = jnp.stack(
            [sums_one[0], sums_one[1], sums_two[2], sums_two[0], sums_two[1], gate_two_grad]
        )
        if layer == 1:
            parts = g.reshape(2, 2, 5, 8, 8, width).transpose(2, 0, 3, 1, 4, 5).reshape(5, 2, 128, width)
            kept = jnp.concatenate(
                [parts[:2].reshape(4, 128, width), either(low_side, parts[2, 0], parts[2, 1])[None]]
            )
            sent = jnp.concatenate(
                [parts[3:].reshape(4, 128, width), either(low_side, parts[2, 1], parts[2, 0])[None]]
            )
            got = swap_side(after(sent.astype(bf16), in_got, out_got)).astype(f32)
            g = jnp.stack(in_order(low_side, kept, got), axis=1).reshape(rows, width)
            first_sums = lax.psum((down_sum, up_sum, last), chip_axes)
            waiting = (last,)
        rows_by_side = table_rows.reshape(6, 2, half)

        def packed(place, acc, pieces):
            return jnp.concatenate(
                [
                    lax.dynamic_index_in_dim(rows_by_side, place, 1, keepdims=False).reshape(-1),
                    table_grad(acc, *maps[layer]).reshape(-1),
                ]
                + [part.reshape(-1) for part in in_order(first_core, pieces[0][2], pieces[1][2])]
            )

        collected[layer] = (packed(side, own_acc, own), packed(1 - side, far_acc, far))

    small = jnp.concatenate([collected[0][0], collected[1][0]])
    small += swap_side(jnp.concatenate([collected[0][1], collected[1][1]]))
    spread = gather_dp(jnp.concatenate([small, activated.astype(f32)]))
    modulation_rows, offset_sums, bias_sums, start = [], [], [], 0
    for layer in range(2):
        modulation_rows.append(spread[:, start : start + 6 * half].reshape(-1, 6, half))
        start += 6 * half
        heads, levels = tables[layer].shape[0] // 2, tables[layer].shape[1]
        offset_sums.append(
            jnp.sum(spread[:, start : start + heads * levels], axis=0).reshape(heads, levels)
        )
        start += heads * levels
        bias_sums.append(jnp.sum(spread[:, start : start + up_bias.shape[1]], axis=0))
        start += up_bias.shape[1]
    modulation_rows = jnp.stack(modulation_rows).transpose(0, 2, 1, 3)

    parts = g.reshape(5, 2, 128, width)
    kept = lax.dynamic_index_in_dim(parts[4], side, 0, keepdims=False).reshape(8, 16, width)
    sent = lax.dynamic_index_in_dim(parts[4], 1 - side, 0, keepdims=False).reshape(8, 16, width)
    shared = jnp.stack(in_order(low_side, kept, swap_side(sent)), axis=1).reshape(-1, width)
    whole = parts[:4].reshape(2, 2, 16, 16, width).transpose(0, 2, 1, 3, 4).reshape(-1, width)
    grad_tokens = either(
        low_side, jnp.concatenate([whole, shared], axis=0), jnp.concatenate([shared, whole], axis=0)
    )

    for _ in range(3):
        advance(g, "last")
    quarters = []
    for layer in range(2):
        parts = dict(zip(("down", "up", "last"), map(both_cores, (second_sums, first_sums)[layer])))
        if layer == 0:
            parts["last"] = both_quarters(*sums[0]["last"][0])
        quarters.append(
            (
                [part[:cut].reshape(in_sum.shape) for part in parts["last"]],
                [part[cut:].reshape(out_sum.shape) for part in parts["last"]],
                parts["up"],
                parts["down"],
            )
        )

    def pair_of(number, axis):
        return jnp.stack(
            [jnp.concatenate(quarters[layer][number], axis=axis).astype(f32) for layer in range(2)]
        )

    return (
        result,
        grad_tokens,
        modulation_back(spots, spread[:, start:], modulation_rows).transpose(0, 2, 1, 3),
        jnp.sum(modulation_rows, axis=2),
        pair_of(0, 2).transpose(0, 2, 1, 3),
        pair_of(1, 0),
        offset_sums[0],
        offset_sums[1],
        pair_of(2, 1),
        jnp.stack(bias_sums),
        pair_of(3, 0),
    )


def solution(mesh):
    chips, odd = divmod(mesh.shape["dp"], 2)
    if mesh.shape["mp"] == 2 and not odd and chips > 1 and chips & (chips - 1) == 0:
        dp, run = ("z", "y", "core"), per_device_pair
        mesh = Mesh(mesh.devices.reshape(-1, 2, 2, 2), dp + ("mp",))
    else:
        dp, run = ("dp",), per_device
    both = dp + ("mp",)
    return jax.shard_map(
        run,
        mesh=mesh,
        in_specs=(
            P(both, None),
            P(both, None),
            P(dp),
            P(dp),
            P(dp),
            P(),
            P(),
            P(None, None, None, "mp"),
            P(None, None, "mp"),
            P(None, None, None, "mp"),
            P(None, "mp", None),
            P("mp", None),
            P("mp", None),
            P(None, None, "mp"),
            P(None, "mp"),
            P(None, "mp", None),
        ),
        out_specs=(
            P(both, None),
            P(both, None),
            P(None, None, None, "mp"),
            P(None, None, "mp"),
            P(None, None, None, "mp"),
            P(None, "mp", None),
            P("mp", None),
            P("mp", None),
            P(None, None, "mp"),
            P(None, "mp"),
            P(None, "mp", None),
        ),
        check_vma=False,
    )
```

```python
import functools

import jax
import jax.numpy as jnp
import numpy as np
from jax import lax
from jax.experimental import pallas as pl
from jax.experimental.pallas import tpu as pltpu
from jax.sharding import Mesh
from jax.sharding import PartitionSpec as P

FRAMES = 5
HEIGHT = 16
WIDTH = 32


HIGH = lax.Precision.HIGHEST
EPSILON = 1e-06
CONTRACT_LAST = (((1,), (1,)), ((), ()))
CONTRACT_FIRST = (((0,), (0,)), ((), ()))


def carried_in(value, axis, join, neutral):
    count, mine = (lax.axis_size(axis), lax.axis_index(axis))
    pieces = lax.all_gather(value, axis)
    total = jnp.full_like(value, 0) + jnp.asarray(neutral, value.dtype)

    def lap(position, total):
        longer = join(total, pieces[position])
        return jnp.where(position < mine, longer, total)

    return lax.fori_loop(0, count - 1, lap, total)


def as_sent(shard):
    return jax.tree.map(lambda a: a.astype(jnp.bfloat16) if a.dtype == jnp.float32 else a, shard)


def normalize(values):
    centred = values - jnp.mean(values, axis=-1, keepdims=True)
    spread = jnp.mean(centred * centred, axis=-1, keepdims=True)
    return centred * lax.rsqrt(spread + EPSILON)


def modulate(values, shift, scale):
    return normalize(values) * (1.0 + scale) + shift


def window_shape(layer):
    if layer == 0:
        return (1, 16, 16)
    return (FRAMES, 8, 8)


def to_windows(values, layer):
    chans = values.shape[-1]
    if layer == 0:
        grid = values.reshape(FRAMES, HEIGHT // 16, 16, WIDTH // 16, 16, chans)
        return grid.transpose(0, 1, 3, 2, 4, 5).reshape(-1, 256, chans)
    grid = values.reshape(FRAMES, HEIGHT // 8, 8, WIDTH // 8, 8, chans)
    return grid.transpose(1, 3, 0, 2, 4, 5).reshape(-1, FRAMES * 64, chans)


def from_windows(values, layer):
    chans = values.shape[-1]
    if layer == 0:
        grid = values.reshape(FRAMES, HEIGHT // 16, WIDTH // 16, 16, 16, chans)
        return grid.transpose(0, 1, 3, 2, 4, 5).reshape(-1, chans)
    grid = values.reshape(HEIGHT // 8, WIDTH // 8, FRAMES, 8, 8, chans)
    return grid.transpose(2, 0, 3, 1, 4, 5).reshape(-1, chans)


def offset_map(layer):
    extents = window_shape(layer)
    count = extents[0] * extents[1] * extents[2]
    place = jnp.arange(count, dtype=jnp.int32)
    positions = (
        place // (extents[1] * extents[2]),
        place // extents[2] % extents[1],
        place % extents[2],
    )
    columns = []
    for position, extent in zip(positions, extents):
        if extent > 1:
            offset = (position[:, None] - position[None, :] + extent - 1).reshape(-1)
            levels = jnp.arange(2 * extent - 1, dtype=jnp.int32)
            columns.append((offset[:, None] == levels[None, :]).astype(jnp.float32))
    return jnp.concatenate(columns, axis=1)


def window_scores(projected, offsets, onehot, layer):
    windows = to_windows(projected, layer)
    count = windows.shape[1]
    heads = offsets.shape[0]
    split = windows.reshape(windows.shape[0], count, 3, heads, -1)
    queries = split[:, :, 0]
    keys = split[:, :, 1]
    values = split[:, :, 2]
    factor = split.shape[-1] ** (-0.5)
    bias = jnp.dot(offsets, onehot.T, precision=HIGH).reshape(heads, count, count)
    scores = (
        jnp.einsum("nqhe,nkhe->nhqk", queries, keys, preferred_element_type=jnp.float32) * factor
        + bias
    )
    return (queries, keys, values, scores, factor)


def gather_rows(values):
    return lax.all_gather(values, "mp", axis=0, tiled=True)


def gather_grads(values):
    return lax.all_gather(values, "mp", axis=0, tiled=True)


def scatter_rows(source, weight, count):

    def term(start, size):
        return jnp.dot(source, weight, preferred_element_type=jnp.float32)

    return lax.psum_scatter(
        term(jnp.int32(0), count * lax.axis_size("mp")), "mp", scatter_dimension=0, tiled=True
    )


def scatter_back(source, weight, count):

    def term(start, size):
        return lax.dot_general(source, weight, CONTRACT_LAST, preferred_element_type=jnp.float32)

    return lax.psum_scatter(
        term(jnp.int32(0), count * lax.axis_size("mp")).astype(jnp.bfloat16),
        "mp",
        scatter_dimension=0,
        tiled=True,
    ).astype(jnp.float32)


def per_device(
    tokens,
    cotangent,
    group_start,
    band_index,
    class_label,
    time_table,
    class_table,
    modulation_weight,
    modulation_bias,
    input_weight,
    output_weight,
    space_offsets,
    time_offsets,
    up_weight,
    up_bias,
    down_weight,
):
    local_rows = tokens.shape[0]
    marked = jnp.where(group_start > 0, band_index, -1)

    def latest(earlier, later):
        return jnp.where(later >= 0, later, earlier)

    before = carried_in(marked, "dp", latest, jnp.full_like(marked, -1))
    current = jnp.where(group_start > 0, band_index, before)
    band_hot = (
        current[:, None] == jnp.arange(time_table.shape[0], dtype=jnp.int32)[None, :]
    ).astype(jnp.float32)
    class_hot = (
        class_label[:, None] == jnp.arange(class_table.shape[0], dtype=jnp.int32)[None, :]
    ).astype(jnp.float32)
    condition = jnp.dot(band_hot, time_table, precision=HIGH) + jnp.dot(
        class_hot, class_table, precision=HIGH
    )
    activated = jax.nn.silu(condition[0]).astype(jnp.bfloat16)
    local_modulation = (
        jnp.einsum("d,ldcf->lcf", activated, modulation_weight, preferred_element_type=jnp.float32)
        + modulation_bias
    )
    modulation = lax.all_gather(local_modulation, "mp", axis=2, tiled=True)
    tables = (space_offsets, time_offsets)
    width = input_weight.shape[1]
    residual = tokens.astype(jnp.float32)
    saved = []
    for layer in range(2):
        shift_one, scale_one, gate_one, shift_two, scale_two, gate_two = [
            modulation[layer, number] for number in range(6)
        ]
        onehot = offset_map(layer)
        entry = residual
        normed = modulate(entry, shift_one, scale_one).astype(jnp.bfloat16)
        gathered = gather_rows(normed)
        projected = jnp.dot(
            gathered, input_weight[layer].reshape(width, -1), preferred_element_type=jnp.float32
        ).astype(jnp.bfloat16)
        queries, keys, values, scores, factor = window_scores(
            projected, tables[layer], onehot, layer
        )
        top = jnp.max(scores, axis=-1, keepdims=True)
        expo = jnp.exp(scores - top)
        total = jnp.sum(expo, axis=-1, keepdims=True)
        probs = (expo / total).astype(jnp.bfloat16)
        mixed = jnp.einsum("nhqk,nkhe->nqhe", probs, values, preferred_element_type=jnp.float32)
        attended = from_windows(
            mixed.reshape(mixed.shape[0], mixed.shape[1], -1).astype(jnp.bfloat16), layer
        )
        branch = scatter_rows(attended, output_weight[layer], local_rows)
        middle = entry + gate_one * branch
        normed_two = modulate(middle, shift_two, scale_two).astype(jnp.bfloat16)
        gathered_two = gather_rows(normed_two)
        hidden_pre = (
            jnp.dot(gathered_two, up_weight[layer], preferred_element_type=jnp.float32)
            + up_bias[layer]
        )
        hidden = jax.nn.gelu(hidden_pre).astype(jnp.bfloat16)
        branch_two = scatter_rows(hidden, down_weight[layer], local_rows)
        residual = middle + gate_two * branch_two
        saved.append(
            (
                entry,
                normed,
                gathered,
                projected,
                top,
                total,
                attended,
                branch,
                middle,
                normed_two,
                gathered_two,
                hidden_pre,
                hidden,
                branch_two,
            )
        )
    grad = cotangent.astype(jnp.float32)
    collected = [None, None]
    for layer in (1, 0):
        (
            entry,
            normed,
            gathered,
            projected,
            top,
            total,
            attended,
            branch,
            middle,
            normed_two,
            gathered_two,
            hidden_pre,
            hidden,
            branch_two,
        ) = saved[layer]
        shift_one, scale_one, gate_one, shift_two, scale_two, gate_two = [
            modulation[layer, number] for number in range(6)
        ]
        onehot = offset_map(layer)
        grad_down_branch = (gate_two * grad).astype(jnp.bfloat16)
        gate_two_grad = jnp.sum(grad * branch_two, axis=0)
        full_down = gather_grads(grad_down_branch)
        grad_hidden = lax.dot_general(
            full_down, down_weight[layer], CONTRACT_LAST, preferred_element_type=jnp.float32
        )
        down_grad = lax.dot_general(
            hidden, full_down, CONTRACT_FIRST, preferred_element_type=jnp.float32
        )
        gelu_pull = jax.vjp(jax.nn.gelu, hidden_pre)[1]
        grad_pre = gelu_pull(grad_hidden)[0].astype(jnp.bfloat16)
        up_bias_grad = jnp.sum(grad_pre, axis=0, dtype=jnp.float32)
        up_grad = lax.dot_general(
            gathered_two, grad_pre, CONTRACT_FIRST, preferred_element_type=jnp.float32
        )
        grad_normed_two = scatter_back(grad_pre, up_weight[layer], local_rows)
        middle_pull = jax.vjp(modulate, middle, shift_two, scale_two)[1]
        grad_middle, shift_two_grad, scale_two_grad = middle_pull(grad_normed_two)
        grad_middle = grad + grad_middle
        grad_out_branch = (gate_one * grad_middle).astype(jnp.bfloat16)
        gate_one_grad = jnp.sum(grad_middle * branch, axis=0)
        full_out = gather_grads(grad_out_branch)
        grad_attended = lax.dot_general(
            full_out, output_weight[layer], CONTRACT_LAST, preferred_element_type=jnp.float32
        ).astype(jnp.bfloat16)
        out_grad = lax.dot_general(
            attended, full_out, CONTRACT_FIRST, preferred_element_type=jnp.float32
        )
        queries, keys, values, scores, factor = window_scores(
            projected, tables[layer], onehot, layer
        )
        probs = jnp.exp(scores - top) / total
        heads = tables[layer].shape[0]
        upstream = to_windows(grad_attended, layer).reshape(queries.shape)
        grad_probs = jnp.einsum(
            "nqhe,nkhe->nhqk", upstream, values, preferred_element_type=jnp.float32
        )
        inner = jnp.sum(probs * grad_probs, axis=-1, keepdims=True)
        grad_scores = (probs * (grad_probs - inner)).astype(jnp.bfloat16)
        offset_grad = jnp.dot(
            jnp.sum(grad_scores, axis=0, dtype=jnp.float32).reshape(heads, -1),
            onehot,
            precision=HIGH,
        )
        grad_queries = (
            jnp.einsum("nhqk,nkhe->nqhe", grad_scores, keys, preferred_element_type=jnp.float32)
            * factor
        ).astype(jnp.bfloat16)
        grad_keys = (
            jnp.einsum("nhqk,nqhe->nkhe", grad_scores, queries, preferred_element_type=jnp.float32)
            * factor
        ).astype(jnp.bfloat16)
        grad_values = jnp.einsum(
            "nhqk,nqhe->nkhe",
            probs.astype(jnp.bfloat16),
            upstream,
            preferred_element_type=jnp.float32,
        ).astype(jnp.bfloat16)
        stacked = jnp.stack([grad_queries, grad_keys, grad_values], axis=2)
        grad_projected = from_windows(
            stacked.reshape(stacked.shape[0], stacked.shape[1], -1), layer
        )
        in_grad = lax.dot_general(
            gathered, grad_projected, CONTRACT_FIRST, preferred_element_type=jnp.float32
        ).reshape(input_weight.shape[1:])
        grad_normed = scatter_back(
            grad_projected, input_weight[layer].reshape(width, -1), local_rows
        )
        entry_pull = jax.vjp(modulate, entry, shift_one, scale_one)[1]
        grad_entry, shift_one_grad, scale_one_grad = entry_pull(grad_normed)
        grad = grad_middle + grad_entry
        partial_rows = jnp.stack(
            [
                shift_one_grad,
                scale_one_grad,
                gate_one_grad,
                shift_two_grad,
                scale_two_grad,
                gate_two_grad,
            ]
        )
        modulation_grad = lax.psum_scatter(partial_rows, "mp", scatter_dimension=1, tiled=True)
        projection_grad = activated.astype(jnp.float32)[:, None, None] * modulation_grad[None]
        grads_here = (
            projection_grad,
            modulation_grad,
            in_grad,
            out_grad,
            offset_grad,
            up_grad,
            up_bias_grad,
            down_grad,
        )
        collected[layer] = grads_here
    summed = jax.tree.map(
        lambda part: part.astype(jnp.float32), lax.psum(as_sent(collected[0] + collected[1]), "dp")
    )
    collected = [summed[:8], summed[8:]]

    def stacked_pair(number):
        return jnp.stack([collected[0][number], collected[1][number]])

    return (
        residual,
        grad,
        stacked_pair(0),
        stacked_pair(1),
        stacked_pair(2),
        stacked_pair(3),
        collected[0][4],
        collected[1][4],
        stacked_pair(5),
        stacked_pair(6),
        stacked_pair(7),
    )


VMEM = 58 * 2**20
COST_SHARE = 64
ROWS = 256
HEAD = 64


def full_block(*shape):
    return pl.BlockSpec(shape, lambda *_: (0,) * len(shape))


def once_block(*shape):
    return pl.BlockSpec(shape, lambda *_: (0,) * len(shape), pipeline_mode=pl.Buffered(1))


def params():
    return pltpu.CompilerParams(vmem_limit_bytes=VMEM)


def cost(flops, moved, exps=0):
    return pl.CostEstimate(
        flops=int(flops) // COST_SHARE,
        bytes_accessed=int(moved) // COST_SHARE,
        transcendentals=int(exps) // COST_SHARE,
    )


def shaped(*arrays):
    return sum(int(np.prod(a.shape)) * a.dtype.itemsize for a in arrays)


def row_norm(values):
    centred = values - jnp.mean(values, axis=-1, keepdims=True)
    spread = jnp.mean(centred * centred, axis=-1, keepdims=True)
    scale = lax.rsqrt(spread + EPSILON)
    return centred * scale, scale


def norm_back(values, grad, shift_scale):
    unit, inverse = row_norm(values)
    inner = grad * (1.0 + shift_scale)
    first = jnp.mean(inner, axis=-1, keepdims=True)
    second = jnp.mean(inner * unit, axis=-1, keepdims=True)
    pulled = inverse * (inner - first - unit * second)
    return (
        pulled,
        jnp.sum(grad, axis=0, keepdims=True),
        jnp.sum(grad * unit, axis=0, keepdims=True),
    )


def call(kernel, name, grid, in_specs, out_specs, out_shape, flops, exps=0, scratch=()):
    def run(spots, *operands):
        moved = shaped(*operands, *jax.tree.leaves(out_shape))
        return pl.pallas_call(
            kernel,
            out_shape=out_shape,
            grid_spec=pltpu.PrefetchScalarGridSpec(
                num_scalar_prefetch=1,
                grid=grid,
                in_specs=in_specs,
                out_specs=out_specs,
                scratch_shapes=scratch,
            ),
            compiler_params=params(),
            cost_estimate=cost(flops, min(moved, 64 * 2**20), exps),
            name=name,
        )(spots, *operands)

    return run


def project_kernel(_, x_ref, shift_ref, scale_ref, weight_ref, turned_ref, normed_ref, out_ref):
    rows = x_ref.shape[0]

    @pl.when(pl.program_id(0) == 0)
    def _():
        for start in range(0, rows, ROWS):
            part = pl.ds(start, ROWS)
            unit, _ = row_norm(x_ref[part, :])
            value = (unit * (1.0 + scale_ref[...]) + shift_ref[...]).astype(jnp.bfloat16)
            normed_ref[part, :] = value
            turned_ref[:, part] = value.T

    project_rows(normed_ref, weight_ref, out_ref)


def side_by_side(ref):
    return jnp.concatenate([ref[0, part] for part in range(3)], axis=1)


def project_more_kernel(_, normed_ref, mine_ref, sib_ref, out_ref):
    @pl.when(pl.program_id(0) == 0)
    def _():
        project_rows(normed_ref, mine_ref, out_ref)

    @pl.when(pl.program_id(0) == 1)
    def _():
        project_rows(normed_ref, sib_ref, out_ref)


def project_rows(normed_ref, weight_ref, out_ref):
    weight = side_by_side(weight_ref)
    for start in range(0, normed_ref.shape[0], ROWS):
        part = pl.ds(start, ROWS)
        out_ref[0, part, :] = jnp.dot(
            normed_ref[part, :], weight, preferred_element_type=jnp.float32
        ).astype(jnp.bfloat16)


def in_spec(layer, width, cols, order):
    return pl.BlockSpec((1, 3, width, cols // 3), lambda *a: (layer, 0, 0, a[-1][order(*a[:-1])]))


def project(spots, layer, x, shift, scale, weight):
    rows, width = x.shape
    cols = 3 * weight.shape[3] // 2
    return call(
        project_kernel,
        "project",
        (2,),
        [
            once_block(rows, width),
            full_block(1, width),
            full_block(1, width),
            in_spec(layer, width, cols, lambda q: q),
        ],
        (
            full_block(width, rows),
            full_block(rows, width),
            pl.BlockSpec((1, rows, cols), lambda q, s: (q, 0, 0)),
        ),
        (
            jax.ShapeDtypeStruct((width, rows), jnp.bfloat16),
            jax.ShapeDtypeStruct((rows, width), jnp.bfloat16),
            jax.ShapeDtypeStruct((2, rows, cols), jnp.bfloat16),
        ),
        4 * rows * width * cols,
    )(spots, x, shift, scale, weight)


def project_more(spots, normed, mine, sib):
    rows, width = normed.shape
    size = mine.shape[2]
    return call(
        project_more_kernel,
        "project_more",
        (2,),
        [once_block(rows, width), full_block(1, 3, width, size), full_block(1, 3, width, size)],
        pl.BlockSpec((1, rows, 3 * size), lambda q, s: (q, 0, 0)),
        jax.ShapeDtypeStruct((2, rows, 3 * size), jnp.bfloat16),
        12 * rows * width * size,
    )(spots, normed, mine[None], sib[None])


def window_heads(proj_ref, ublk_ref, place, extra_ref=None):
    count = place.shape[0]
    heads = ublk_ref.shape[0]
    wide = heads * HEAD
    lane = lax.broadcasted_iota(jnp.int32, (count, 128), 1)
    items = []
    for window in range(proj_ref.shape[1] // count):
        rows = pl.ds(window * count, count)
        for pair in range(heads // 2):
            cols = pl.ds(pair * 128, 128)
            query, key, value = (
                proj_ref[0, rows, part * wide + pair * 128 : part * wide + pair * 128 + 128]
                for part in range(3)
            )
            kk = jnp.concatenate([key, place], axis=1)
            for half in range(2):
                mine = (lane < HEAD) if half == 0 else (lane >= HEAD)
                scaled = jnp.where(mine, query * HEAD**-0.5, 0.0).astype(jnp.bfloat16)
                above = None
                if extra_ref is not None:
                    above = jnp.where(mine, extra_ref[rows, cols], 0.0).astype(jnp.bfloat16)
                items.append((rows, pair, 2 * pair + half, kk, key, value, scaled, above))
    return items, lane


def head_scores(item, ublk_ref):
    query = jnp.concatenate([item[6], ublk_ref[item[2]]], axis=1)
    return lax.dot_general(item[3], query, CONTRACT_LAST, preferred_element_type=jnp.float32)


def head_probs(scores):
    expo = jnp.exp(scores - jnp.max(scores, axis=0, keepdims=True))
    return expo * (1.0 / jnp.sum(expo, axis=0, keepdims=True))


def ahead(items, first, middle, last):
    ready, count = first(items[0]), len(items)
    held = None
    for i in range(count):
        later = first(items[i + 1]) if i + 1 < count else None
        now = middle(ready)
        if i > 0:
            last(i - 1, held)
        ready, held = later, now
    last(count - 1, held)


def attend_kernel(_, proj_ref, ublk_ref, place_ref, out_ref):
    items, lane = window_heads(proj_ref, ublk_ref, place_ref[...])
    done = []

    def mix(i, probs):
        rows, pair, value = items[i][0], items[i][1], items[i][5]
        done.append(
            lax.dot_general(probs, value, CONTRACT_FIRST, preferred_element_type=jnp.float32)
        )
        if i % 2:
            out_ref[rows, pair * 128 : pair * 128 + 128] = jnp.where(
                lane < HEAD, done[i - 1], done[i]
            ).astype(jnp.bfloat16)

    ahead(
        items,
        lambda item: head_scores(item, ublk_ref),
        lambda scores: head_probs(scores).astype(jnp.bfloat16),
        mix,
    )


def attend(spots, first, proj, ublk, place):
    quarters, rows, cols = proj.shape
    count = place.shape[0]
    heads = ublk.shape[0] // 4
    pairs = rows * count * heads * quarters
    return call(
        attend_kernel,
        "attend",
        (quarters,),
        [
            pl.BlockSpec((1, rows, cols), lambda q, s: (q, 0, 0)),
            pl.BlockSpec((heads, count, 128), lambda q, s: (first + s[q], 0, 0)),
            full_block(count, 128),
        ],
        pl.BlockSpec((rows, heads * HEAD), lambda q, s: (0, q)),
        jax.ShapeDtypeStruct((rows, quarters * heads * HEAD), jnp.bfloat16),
        pairs * 768,
        pairs,
    )(spots, proj, ublk, place)


def join_kernel(
    _, own_ref, far_ref, w0_ref, w1_ref, w2_ref, w3_ref, x_ref, gate_ref, shift_ref, scale_ref,
    branch_ref, middle_ref, normed_ref, turned_ref,
):
    weights = [w0_ref[0], w1_ref[0], w2_ref[...], w3_ref[...]]
    branch = jnp.dot(
        jnp.concatenate([own_ref[...], far_ref[...]], axis=1),
        jnp.concatenate(weights, axis=0),
        preferred_element_type=jnp.float32,
    )
    branch_ref[...] = branch
    middle = x_ref[...] + gate_ref[...] * branch
    middle_ref[...] = middle
    unit, _ = row_norm(middle)
    normed = (unit * (1.0 + scale_ref[...]) + shift_ref[...]).astype(jnp.bfloat16)
    normed_ref[...] = normed
    turned_ref[...] = normed.T


def row_tile(cols):
    return pl.BlockSpec((ROWS, cols), lambda i, s: (i, 0))


def quarter_rows(layer, r, size, width):
    return pl.BlockSpec(
        (1, size, width), lambda i, s: (layer, s[r], 0), pipeline_mode=pl.Buffered(1)
    )


def join(spots, layer, own, far, weight, recv, sib, x, gate, shift, scale):
    rows, width = x.shape
    half = own.shape[1]
    tile = row_tile(width)
    size = half // 2
    return call(
        join_kernel,
        "join",
        (rows // ROWS,),
        [
            row_tile(half),
            row_tile(half),
            quarter_rows(layer, 0, size, width),
            quarter_rows(layer, 1, size, width),
            once_block(size, width),
            once_block(size, width),
            tile,
        ]
        + [full_block(1, width)] * 3,
        (tile, tile, tile, pl.BlockSpec((width, ROWS), lambda i, s: (0, i))),
        (
            jax.ShapeDtypeStruct((rows, width), jnp.float32),
            jax.ShapeDtypeStruct((rows, width), jnp.float32),
            jax.ShapeDtypeStruct((rows, width), jnp.bfloat16),
            jax.ShapeDtypeStruct((width, rows), jnp.bfloat16),
        ),
        2 * rows * width * width,
    )(spots, own, far, weight, weight, recv, sib, x, gate, shift, scale)


SLOPE = float(np.sqrt(2 / np.pi))


def up_kernel(_, normed_ref, weight_ref, bias_ref, pre_ref, hidden_ref):
    starts = list(range(0, normed_ref.shape[0], ROWS))

    def product(start):
        return (
            jnp.dot(
                normed_ref[pl.ds(start, ROWS), :], weight_ref[0], preferred_element_type=jnp.float32
            )
            + bias_ref[0, 0]
        )

    pre = product(starts[0])
    for start, following in zip(starts, starts[1:] + [None]):
        later = None if following is None else product(following)
        part = pl.ds(start, ROWS)
        pre_ref[0, part, :] = pre
        bent = jnp.tanh(pre * (SLOPE + (SLOPE * 0.044715) * (pre * pre)))
        half = 0.5 * pre
        hidden_ref[0, part, :] = (half + half * bent).astype(jnp.bfloat16)
        pre = later


def up_spec(layer, own, width, cols, step, order):
    if own:
        per = cols // step
        return pl.BlockSpec(
            (1, width, step), lambda *a: (layer, 0, a[-1][order(*a[:-1])[0]] * per + order(*a[:-1])[1])
        )
    return pl.BlockSpec((1, width, step), lambda *a: (0, 0, order(*a[:-1])[1]))


def up(spots, layer, quarter, normed, weight, bias):
    rows, width = normed.shape
    cols = bias.shape[3]
    step = cols // 2
    own = quarter is None
    count = 2 if own else 1
    tile = pl.BlockSpec((1, rows, step), lambda q, j, s: (q, 0, j))
    return call(
        up_kernel,
        "up",
        (count, cols // step),
        [
            once_block(rows, width),
            up_spec(layer, own, width, cols, step, lambda q, j: (q, j)),
            pl.BlockSpec((1, 1, 1, step), lambda q, j, s: (layer, s[q if own else quarter], 0, j)),
        ],
        (tile, tile),
        (
            jax.ShapeDtypeStruct((count, rows, cols), jnp.float32),
            jax.ShapeDtypeStruct((count, rows, cols), jnp.bfloat16),
        ),
        2 * count * rows * width * cols,
        count * rows * cols,
    )(spots, normed, weight if own else weight[None], bias)


def down_kernel(
    _, own_ref, far_ref, sib_ref, w0_ref, w1_ref, w2_ref, w3_ref, middle_ref, gate_ref, branch_ref, out_ref
):
    total = jnp.dot(own_ref[0], w0_ref[0], preferred_element_type=jnp.float32)
    total += jnp.dot(own_ref[1], w1_ref[0], preferred_element_type=jnp.float32)
    total += jnp.dot(far_ref[0], w2_ref[...], preferred_element_type=jnp.float32)
    total += jnp.dot(sib_ref[0], w3_ref[...], preferred_element_type=jnp.float32)
    branch_ref[...] = total
    out_ref[...] = middle_ref[...] + gate_ref[...] * total


def down(spots, layer, own, far, far_sib, weight, recv, sib, middle, gate):
    rows, width = middle.shape
    cols = own.shape[2]
    tile = row_tile(width)
    hidden, single = (pl.BlockSpec((n, ROWS, cols), lambda i, s: (0, i, 0)) for n in (2, 1))
    return call(
        down_kernel,
        "down",
        (rows // ROWS,),
        [
            hidden,
            single,
            single,
            quarter_rows(layer, 0, cols, width),
            quarter_rows(layer, 1, cols, width),
            once_block(cols, width),
            once_block(cols, width),
            tile,
            full_block(1, width),
        ],
        (tile, tile),
        (
            jax.ShapeDtypeStruct((rows, width), jnp.float32),
            jax.ShapeDtypeStruct((rows, width), jnp.float32),
        ),
        8 * rows * width * cols,
    )(spots, own, far, far_sib, weight, weight, recv, sib, middle, gate)


def feed_back_kernel(
    _, gdb_ref, hidden_ref, pre_ref, turned_ref, down_ref, up_ref,
    down_grad_ref, up_grad_ref, bias_grad_ref, normed_grad_ref, gpre_ref, total_ref,
):
    starts = list(range(0, gdb_ref.shape[0], ROWS))
    columns = gdb_ref.shape[1] // 4
    sums = jnp.zeros(bias_grad_ref.shape, jnp.float32)

    def product(start):
        return lax.dot_general(
            gdb_ref[pl.ds(start, ROWS), :], down_ref[0], CONTRACT_LAST, preferred_element_type=jnp.float32
        )

    grad_hidden = product(starts[0])
    for i, start in enumerate(starts):
        later = product(starts[i + 1]) if i + 1 < len(starts) else None
        if i < 4:
            part = pl.ds(i * columns, columns)
            down_grad_ref[:, part] = lax.dot_general(
                hidden_ref[0], gdb_ref[:, part], CONTRACT_FIRST, preferred_element_type=jnp.float32
            ).astype(jnp.bfloat16)
        part = pl.ds(start, ROWS)
        pre = pre_ref[0, part, :]
        square = pre * pre
        bent = jnp.tanh(pre * (SLOPE + (SLOPE * 0.044715) * square))
        half = 0.5 + 0.5 * bent
        slope = half + (pre * (half * (1.0 - bent))) * (SLOPE + (3 * 0.044715 * SLOPE) * square)
        grad_pre = (grad_hidden * slope).astype(jnp.bfloat16)
        gpre_ref[part, :] = grad_pre
        sums += jnp.sum(grad_pre.astype(jnp.float32), axis=0, keepdims=True)
        grad_hidden = later
    bias_grad_ref[...] = sums
    up_grad_ref[...] = jnp.dot(
        turned_ref[...], gpre_ref[...], preferred_element_type=jnp.float32
    ).astype(jnp.bfloat16)

    def each(store):
        for start in starts:
            part = pl.ds(start, ROWS)
            term = lax.dot_general(
                gpre_ref[part, :], up_ref[0], CONTRACT_LAST, preferred_element_type=jnp.float32
            )
            store(part, term)

    step, steps = pl.program_id(0), pl.num_programs(0)

    @pl.when(step == 0)
    def _():
        def store(part, term):
            total_ref[part, :] = term

        each(store)

    @pl.when(step == steps - 1)
    def _():
        def store(part, term):
            normed_grad_ref[part, :] = (total_ref[part, :] + term).astype(jnp.bfloat16)

        each(store)


def feed_back(spots, layer, own, r, gdb, hidden, pre, turned, down_weight, up_weight):
    rows, width = gdb.shape
    cols = hidden.shape[2]
    step = cols // 2
    per = cols // step
    if own:
        down_spec = pl.BlockSpec((1, step, width), lambda j, s: (layer, s[r] * per + j, 0))
    else:
        down_weight, up_weight = down_weight[None], up_weight[None]
        down_spec = pl.BlockSpec((1, step, width), lambda j, s: (0, j, 0))
    return call(
        feed_back_kernel,
        "feed_back",
        (per,),
        [
            once_block(rows, width),
            pl.BlockSpec((1, rows, step), lambda j, s: (r if own else 0, 0, j)),
            pl.BlockSpec((1, rows, step), lambda j, s: (r if own else 0, 0, j)),
            once_block(width, rows),
            down_spec,
            up_spec(layer, own, width, cols, step, lambda j: (r, j)),
        ],
        (
            pl.BlockSpec((step, width), lambda j, s: (j, 0)),
            pl.BlockSpec((width, step), lambda j, s: (0, j)),
            pl.BlockSpec((1, step), lambda j, s: (0, j)),
            full_block(rows, width),
        ),
        (
            jax.ShapeDtypeStruct((cols, width), jnp.bfloat16),
            jax.ShapeDtypeStruct((width, cols), jnp.bfloat16),
            jax.ShapeDtypeStruct((1, cols), jnp.float32),
            jax.ShapeDtypeStruct((rows, width), jnp.bfloat16),
        ),
        8 * rows * width * cols,
        rows * cols,
        scratch=[pltpu.VMEM((rows, step), jnp.bfloat16), pltpu.VMEM((rows, width), jnp.float32)],
    )(spots, gdb, hidden, pre, turned, down_weight, up_weight)


def join_back_kernel(
    _, one_ref, two_ref, three_ref, four_ref, g_ref, middle_ref, branch_ref, own_ref, far_ref,
    w0_ref, w1_ref, w2_ref, w3_ref, gate_ref, scale_ref,
    grad_middle_ref, grad_own_ref, grad_far_ref, own_grad_ref, far_grad_ref, sums_ref, total_ref,
):
    one, two, three, four = (
        ref[...].astype(jnp.float32) for ref in (one_ref, two_ref, three_ref, four_ref)
    )
    partial = (one + two) + (three + four)
    pulled, shift_sum, scale_sum = norm_back(middle_ref[...], partial, scale_ref[...])
    grad_middle = g_ref[...] + pulled
    grad_middle_ref[...] = grad_middle
    gate_sum = jnp.sum(grad_middle * branch_ref[...], axis=0, keepdims=True)
    grad_branch = (gate_ref[...] * grad_middle).astype(jnp.bfloat16)
    weights = jnp.concatenate([w0_ref[0], w1_ref[0], w2_ref[...], w3_ref[...]], axis=0)
    grad_att = lax.dot_general(
        grad_branch, weights, CONTRACT_LAST, preferred_element_type=jnp.float32
    ).astype(jnp.bfloat16)
    half = own_ref.shape[1]
    grad_own_ref[...] = grad_att[:, :half]
    grad_far_ref[...] = grad_att[:, half:]
    att = jnp.concatenate([own_ref[...], far_ref[...]], axis=1)
    weight_term = lax.dot_general(
        att, grad_branch, CONTRACT_FIRST, preferred_element_type=jnp.float32
    )
    sums = jnp.concatenate([shift_sum, scale_sum, gate_sum], axis=0)
    step = pl.program_id(0)

    @pl.when(step == 0)
    def _():
        total_ref[...] = weight_term
        sums_ref[...] = sums

    @pl.when(step > 0)
    def _():
        total_ref[...] += weight_term
        sums_ref[...] += sums

    @pl.when(step == pl.num_programs(0) - 1)
    def _():
        own_grad_ref[...] = total_ref[:half, :].astype(jnp.bfloat16)
        far_grad_ref[...] = total_ref[half:, :].astype(jnp.bfloat16)


def join_back(spots, layer, partials, g, middle, branch, own, far, weight, recv, sib, gate, scale):
    rows, width = g.shape
    half = own.shape[1]
    size = half // 2
    tile = row_tile(width)
    return call(
        join_back_kernel,
        "join_back",
        (rows // ROWS,),
        [tile] * 7
        + [
            row_tile(half),
            row_tile(half),
            quarter_rows(layer, 0, size, width),
            quarter_rows(layer, 1, size, width),
            once_block(size, width),
            once_block(size, width),
        ]
        + [full_block(1, width)] * 2,
        (
            tile,
            row_tile(half),
            row_tile(half),
            full_block(half, width),
            full_block(half, width),
            full_block(3, width),
        ),
        (
            jax.ShapeDtypeStruct((rows, width), jnp.float32),
            jax.ShapeDtypeStruct((rows, half), jnp.bfloat16),
            jax.ShapeDtypeStruct((rows, half), jnp.bfloat16),
            jax.ShapeDtypeStruct((half, width), jnp.bfloat16),
            jax.ShapeDtypeStruct((half, width), jnp.bfloat16),
            jax.ShapeDtypeStruct((3, width), jnp.float32),
        ),
        4 * rows * width * width,
        scratch=[pltpu.VMEM((width, width), jnp.float32)],
    )(spots, *partials, g, middle, branch, own, far, weight, weight, recv, sib, gate, scale)


def attend_back_kernel(_, proj_ref, grad_ref, ublk_ref, place_ref, out_ref, table_ref):
    place = place_ref[...]
    items, lane = window_heads(proj_ref, ublk_ref, place, grad_ref)
    wide = ublk_ref.shape[0] * HEAD
    tables = {}
    done = []

    def first(item):
        grad_probs = lax.dot_general(
            item[5], item[7], CONTRACT_LAST, preferred_element_type=jnp.float32
        )
        return head_scores(item, ublk_ref), grad_probs

    def middle(pair):
        probs, grad_probs = head_probs(pair[0]), pair[1]
        inner = jnp.sum(probs * grad_probs, axis=0, keepdims=True)
        return probs.astype(jnp.bfloat16), (probs * (grad_probs - inner)).astype(jnp.bfloat16)

    def last(i, held):
        probs, grad_scores = held
        rows, pair, head, _, key, _, scaled, above = items[i]
        both = jnp.dot(
            grad_scores, jnp.concatenate([scaled, place], axis=1), preferred_element_type=jnp.float32
        )
        grad_value = jnp.dot(probs, above, preferred_element_type=jnp.float32)
        grad_query = lax.dot_general(
            grad_scores,
            (key * HEAD**-0.5).astype(jnp.bfloat16),
            CONTRACT_FIRST,
            preferred_element_type=jnp.float32,
        )
        tables[head] = both[:, 128:] if head not in tables else tables[head] + both[:, 128:]
        done.append((grad_query, both[:, :128], grad_value))
        if i % 2:
            (q0, k0, v0), (q1, k1, v1) = done[i - 1], done[i]
            for part, value in enumerate((jnp.where(lane < HEAD, q0, q1), k0 + k1, v0 + v1)):
                out_ref[0, rows, part * wide + pair * 128 : part * wide + pair * 128 + 128] = (
                    value.astype(jnp.bfloat16)
                )

    ahead(items, first, middle, last)
    for head, value in tables.items():
        table_ref[head] = value


def attend_back(spots, first, proj, grad, ublk, place):
    quarters, rows, cols = proj.shape
    count = place.shape[0]
    heads = ublk.shape[0] // 4
    pairs = rows * count * heads * quarters
    return call(
        attend_back_kernel,
        "attend_back",
        (quarters,),
        [
            pl.BlockSpec((1, rows, cols), lambda q, s: (q, 0, 0)),
            pl.BlockSpec((rows, heads * HEAD), lambda q, s: (0, q)),
            pl.BlockSpec((heads, count, 128), lambda q, s: (first + s[q], 0, 0)),
            full_block(count, 128),
        ],
        (
            pl.BlockSpec((1, rows, cols), lambda q, s: (q, 0, 0)),
            pl.BlockSpec((heads, count, 128), lambda q, s: (s[q], 0, 0)),
        ),
        (
            jax.ShapeDtypeStruct(proj.shape, jnp.bfloat16),
            jax.ShapeDtypeStruct((ublk.shape[0] // 2, count, 128), jnp.float32),
        ),
        pairs * 1536,
        pairs,
    )(spots, proj, grad, ublk, place)


def in_grad_kernel(_, turned_ref, grad_ref, mine_ref, sib_ref):
    def store(ref):
        for part in range(3):
            size = ref.shape[2]
            ref[part] = jnp.dot(
                turned_ref[...],
                grad_ref[0, :, part * size : part * size + size],
                preferred_element_type=jnp.float32,
            ).astype(jnp.bfloat16)

    @pl.when(pl.program_id(0) == 0)
    def _():
        store(sib_ref)

    @pl.when(pl.program_id(0) == 1)
    def _():
        store(mine_ref)


def in_grad(spots, turned, grad):
    width, rows = turned.shape
    cols = grad.shape[2]
    size = cols // 3
    out = jax.ShapeDtypeStruct((3, width, size), jnp.bfloat16)
    return call(
        in_grad_kernel,
        "in_grad",
        (2, 2),
        [
            pl.BlockSpec((width // 2, rows), lambda q, j, s: (j, 0)),
            pl.BlockSpec((1, rows, cols), lambda q, j, s: (1 - q, 0, 0)),
        ],
        (
            pl.BlockSpec((3, width // 2, size), lambda q, j, s: (0, q * j, 0)),
            pl.BlockSpec((3, width // 2, size), lambda q, j, s: (0, jnp.maximum(q, j), 0)),
        ),
        (out, out),
        4 * rows * width * cols,
    )(spots, turned, grad)


def project_back_kernel(
    _, own_ref, far_ref, w0_ref, w1_ref, w2_ref, w3_ref, x_ref, middle_ref, scale_ref, out_ref, sums_ref
):
    total = None
    for grad, weight in (
        (own_ref[0], w0_ref), (own_ref[1], w1_ref), (far_ref[0], w2_ref), (far_ref[1], w3_ref)
    ):
        term = lax.dot_general(
            grad, side_by_side(weight), CONTRACT_LAST, preferred_element_type=jnp.float32
        )
        total = term if total is None else total + term
    pulled, shift_sum, scale_sum = norm_back(x_ref[...], total, scale_ref[...])
    out_ref[...] = middle_ref[...] + pulled
    sums = jnp.concatenate([shift_sum, scale_sum], axis=0)

    @pl.when(pl.program_id(0) == 0)
    def _():
        sums_ref[...] = sums

    @pl.when(pl.program_id(0) > 0)
    def _():
        sums_ref[...] += sums


def project_back(spots, layer, own, far, weight, mine, sib, x, grad_middle, scale):
    rows, width = x.shape
    cols = own.shape[2]
    tile = row_tile(width)
    grad = pl.BlockSpec((2, ROWS, cols), lambda i, s: (0, i, 0))

    return call(
        project_back_kernel,
        "project_back",
        (rows // ROWS,),
        [grad, grad]
        + [in_spec(layer, width, cols, lambda i, r=r: r) for r in (0, 1)]
        + [full_block(1, 3, width, cols // 3)] * 2
        + [tile, tile, full_block(1, width)],
        (tile, full_block(2, width)),
        (
            jax.ShapeDtypeStruct((rows, width), jnp.float32),
            jax.ShapeDtypeStruct((2, width), jnp.float32),
        ),
        8 * rows * width * cols,
    )(spots, own, far, weight, weight, mine[None], sib[None], x, grad_middle, scale)


def modulation_kernel(_, activated_ref, rows_ref, out_ref):
    out_ref[0, 0] = lax.dot_general(
        activated_ref[...], rows_ref[0, 0], CONTRACT_FIRST, preferred_element_type=jnp.float32
    )


def modulation_back(spots, activated, rows):
    layers, kinds, _, cols = rows.shape
    count, width = activated.shape
    values = jnp.concatenate(split_bits(rows), axis=2)
    return call(
        modulation_kernel,
        "modulation_back",
        (layers, kinds),
        [
            full_block(3 * count, width),
            pl.BlockSpec((1, 1, 3 * count, cols), lambda l, k, s: (l, k, 0, 0)),
        ],
        pl.BlockSpec((1, 1, width, cols), lambda l, k, s: (l, k, 0, 0)),
        jax.ShapeDtypeStruct((layers, kinds, width, cols), jnp.float32),
        6 * layers * kinds * count * width * cols,
    )(spots, jnp.concatenate([activated.astype(jnp.bfloat16)] * 3), values)


SWAP = [(0, 1), (1, 0)]


def either(flag, one, two):
    return jnp.where(flag, one, two)


def split_bits(values):
    parts = []
    for _ in range(3):
        part = lax.reduce_precision(values, 8, 7)
        parts.append(part.astype(jnp.bfloat16))
        values = values - part
    return parts


def place_maps(layer, frames):
    extents = window_shape(layer)
    count = extents[0] * extents[1] * extents[2]
    place = np.arange(count)
    positions = (place // (extents[1] * extents[2]), place // extents[2] % extents[1], place % extents[2])
    hots = []
    width = sum(e for e in extents if e > 1)
    levels = sum(2 * e - 1 for e in extents if e > 1)
    pick = np.zeros((levels, width, width), np.float32)
    column = base = 0
    for position, extent in zip(positions, extents):
        if extent == 1:
            continue
        spots = jnp.asarray(position, jnp.int32)
        if extent == FRAMES and layer == 1:
            spots = frames[spots]
        hots.append((spots[:, None] == jnp.arange(extent, dtype=jnp.int32)[None, :]).astype(jnp.float32))
        for i in range(extent):
            for j in range(extent):
                pick[base + i - j + extent - 1, column + i, column + j] = 1
        column += extent
        base += 2 * extent - 1
    return jnp.concatenate(hots, axis=1), pick


def bias_blocks(table, hot, pick):
    pairs = jnp.einsum("hx,xij->hij", table, pick, precision=HIGH)
    spread = jnp.einsum("ai,hij->haj", hot, pairs, precision=HIGH)
    parts = split_bits(spread)
    room = 128 - 3 * hot.shape[1]
    padded = jnp.concatenate(parts + [jnp.zeros(spread.shape[:2] + (room,), jnp.bfloat16)], axis=2)
    one = hot.astype(jnp.bfloat16)
    place = jnp.concatenate([one] * 3 + [jnp.zeros((hot.shape[0], room), jnp.bfloat16)], axis=1)
    return padded, place


def table_grad(acc, hot, pick):
    width = hot.shape[1]
    pairs = jnp.einsum("hbi,bj->hij", acc[:, :, :width], hot, precision=HIGH)
    return jnp.einsum("hij,xij->hx", pairs, pick, precision=HIGH)


def per_device_pair(
    tokens,
    cotangent,
    group_start,
    band_index,
    class_label,
    time_table,
    class_table,
    modulation_weight,
    modulation_bias,
    input_weight,
    output_weight,
    space_offsets,
    time_offsets,
    up_weight,
    up_bias,
    down_weight,
):
    core = lax.axis_index("core")
    chip_axes = ("z", "y")
    chip = lax.axis_index(chip_axes)
    side = lax.axis_index("mp")
    chips = lax.axis_size(chip_axes)
    low_side, first_core = side == 0, core == 0
    rows, width = tokens.shape
    half = width // 2
    bf16, f32 = jnp.bfloat16, jnp.float32
    spots = jnp.stack([core, 1 - core]).astype(jnp.int32)

    def swap_side(value):
        return lax.ppermute(value, "mp", SWAP)

    def swap_core(value):
        return lax.ppermute(value, "core", SWAP)

    def half_of(value, axis):
        size = value.shape[axis] // 2
        return lax.dynamic_slice_in_dim(value, core * size, size, axis)

    def after(value, *others):
        return lax.optimization_barrier((value,) + others)[0]

    def in_order(flag, one, two):
        return [either(flag, one, two), either(flag, two, one)]

    def gather_dp(value):
        stack = value[None]
        stack = jnp.concatenate(in_order(first_core, stack, swap_core(stack)))
        distance = 1
        while distance < chips:
            got = lax.ppermute(stack, chip_axes, [(i, i ^ distance) for i in range(chips)])
            stack = jnp.concatenate(in_order((chip // distance) % 2 == 0, stack, got))
            distance *= 2
        return stack

    here_y, here_z = lax.axis_index("y"), lax.axis_index("z")
    size_z = lax.axis_size("z")

    def swap_y(value):
        return lax.ppermute(value, "y", SWAP)

    def eighth(value, axis):
        size = value.shape[axis] // 4
        return lax.dynamic_slice_in_dim(value, (2 * core + here_y) * size, size, axis)

    def quarter(got, axis, start=None, use=None):
        got = got if start is None else after(got, start)
        other = swap_y(got)
        other = other if use is None else after(other, use)
        return jnp.concatenate(in_order(here_y == 0, got, other), axis=axis)

    in_weight = input_weight.transpose(0, 2, 1, 3)
    first_piece = eighth(in_weight[0], 2)
    marked = after(jnp.where(group_start > 0, band_index, -1), first_piece)
    every = lax.all_gather(marked, chip_axes + ("core",), tiled=True)
    mine = lax.axis_index(chip_axes + ("core",))
    order = jnp.arange(every.shape[0], dtype=jnp.int32)
    latest = jnp.max(jnp.where((every >= 0) & (order <= mine), order, -1))
    current = jnp.sum(jnp.where(order == latest, every, 0)) + jnp.where(latest < 0, -1, 0)
    band_hot = (current == jnp.arange(time_table.shape[0], dtype=jnp.int32)).astype(f32)
    class_hot = (class_label[0] == jnp.arange(class_table.shape[0], dtype=jnp.int32)).astype(f32)
    condition = jnp.sum(band_hot[:, None] * time_table, axis=0) + jnp.sum(
        class_hot[:, None] * class_table, axis=0
    )
    activated = jax.nn.silu(condition).astype(bf16)
    local_modulation = (
        jnp.einsum("d,ldcf->lcf", activated, modulation_weight, preferred_element_type=f32)
        + modulation_bias
    )
    modulation_got = swap_side(local_modulation)
    modulation = jnp.concatenate(in_order(low_side, local_modulation, modulation_got), axis=2)

    far_in, far_up, far_down = ([None, None] for _ in range(3))
    far_small = swap_side(
        jnp.concatenate([space_offsets.reshape(-1), time_offsets.reshape(-1), up_bias.reshape(-1)])
    )
    cut_one = space_offsets.size
    cut_two = cut_one + time_offsets.size
    tables = (
        jnp.concatenate([space_offsets, far_small[:cut_one].reshape(space_offsets.shape)]),
        jnp.concatenate([time_offsets, far_small[cut_one:cut_two].reshape(time_offsets.shape)]),
    )
    biases = (up_bias.reshape(2, 2, 1, -1), far_small[cut_two:].reshape(2, 2, 1, -1))

    def after_all(values, *others):
        return lax.optimization_barrier((values,) + others)[0]

    def fetch(layer, trigger):
        sources = after_all((in_weight, up_weight, down_weight), trigger)
        return [
            swap_side(eighth(source[layer], axis)) for source, axis in zip(sources, (2, 1, 0))
        ]

    fetched = [fetch(0, modulation_got), None]
    fetched[0][0] = swap_side(first_piece)
    out_got = swap_side(eighth(after(output_weight, modulation_got), 1))
    far_out, far_in, far_up, far_down = ([None, None] for _ in range(4))

    split = lax.dynamic_slice_in_dim(tokens, (1 - side) * (rows - ROWS), ROWS, 0).reshape(8, 2, 16, width)
    kept = lax.dynamic_index_in_dim(split, side, 1, keepdims=False)
    got = swap_side(lax.dynamic_index_in_dim(split, 1 - side, 1, keepdims=False))
    shared = jnp.concatenate(in_order(low_side, kept, got), axis=0)
    whole = lax.dynamic_slice_in_dim(tokens, side * ROWS, rows - ROWS, 0)
    whole = whole.reshape(2, 16, 2, 16, width).transpose(0, 2, 1, 3, 4)
    x = jnp.concatenate([whole.reshape(-1, width), shared.reshape(-1, width)], axis=0).astype(f32)

    frames = jnp.where(
        low_side,
        jnp.asarray([0, 1, 2, 3, 4], jnp.int32),
        jnp.asarray([3, 4, 2, 0, 1], jnp.int32),
    )
    maps = [place_maps(layer, frames) for layer in range(2)]

    def send_cotangent(value):
        chunks = value.reshape(5, ROWS, width)
        return chunks, swap_side(jnp.stack([chunks[1], chunks[3]]))

    def turn_cotangent(chunks, got):
        kept = [
            either(low_side, chunks[0], chunks[2]),
            either(low_side, chunks[2], chunks[4]),
            either(low_side, chunks[4], chunks[0]),
        ]
        ordered = jnp.concatenate([jnp.stack(kept), got]).reshape(5, 8, 4, 8, width)
        return ordered.transpose(2, 0, 1, 3, 4).reshape(rows, width).astype(f32)

    saved = []
    for layer in range(2):
        shift_one, scale_one, gate_one, shift_two, scale_two, gate_two = [
            modulation[layer, number][None] for number in range(6)
        ]
        ublk, place = bias_blocks(tables[layer], *maps[layer])
        turned, normed, own_proj = project(
            spots, layer, x, after(shift_one, far_small, fetched[layer][0]), scale_one, in_weight
        )
        if layer == 0:
            fetched[1] = fetch(1, own_proj)
            out_quarters = quarter(out_got, 1, own_proj)
            far_in[0] = [quarter(fetched[0][0], 2)]
        else:
            far_in[1] = [quarter(fetched[1][0], 2, first_hidden, x)]
        own_att = attend(spots, 0, after(own_proj, far_in[layer][0]), ublk, place)
        far_in[layer].append(swap_core(far_in[layer][0]))
        far_proj = project_more(spots, after(normed, own_att), *far_in[layer])
        far_out[layer] = [out_quarters[layer], swap_core(after(out_quarters, own_att)[layer])]
        far_att = attend(spots, 2, far_proj, ublk, place)
        branch, middle, normed_two, turned_two = join(
            spots, layer, own_att, far_att, output_weight, *far_out[layer], x, gate_one, shift_two, scale_two
        )
        start, use = (far_proj, normed_two) if layer == 0 else (first_hidden, own_proj)
        far_up[layer] = [quarter(fetched[layer][1], 1, start, use)]
        far_down[layer] = [quarter(fetched[layer][2], 0, start, use)]
        for kept in (far_up, far_down):
            kept[layer].append(swap_core(kept[layer][0]))
        if layer == 1:
            chunks, cotangent_got = send_cotangent(after(cotangent, far_att))
        own_pre, own_hidden = up(spots, layer, None, normed_two, up_weight, biases[0])
        far_pre, far_hidden = [None, None], [None, None]
        for r in range(2):
            far_pre[r], far_hidden[r] = up(spots, layer, r, normed_two, far_up[layer][r], biases[1])
        first_hidden = far_hidden[1]
        if layer == 1:
            g = turn_cotangent(chunks, after(cotangent_got, far_hidden[1]))
        if layer == 0:
            far_hidden[1] = after(far_hidden[1], *fetched[1])
        branch_two, out = down(
            spots, layer, own_hidden, *far_hidden, down_weight, *far_down[layer],
            middle if layer == 0 else after(middle, g), gate_two,
        )
        saved.append(
            (
                x, turned, own_proj, far_proj, own_att, far_att, branch, middle, turned_two,
                own_pre, own_hidden, far_pre, far_hidden, branch_two, ublk, place,
            )
        )
        if layer == 0:
            parts = out.reshape(5, 2, 128, width)
            kept = lax.dynamic_index_in_dim(parts, side, 1, keepdims=False)
            sent = lax.dynamic_index_in_dim(parts, 1 - side, 1, keepdims=False).astype(bf16)
            got = swap_side(sent).astype(f32)
            shared = jnp.stack(in_order(low_side, kept[4], got[4]))
            x = jnp.concatenate([kept[:4], shared, got[:4]])
            x = x.reshape(5, 2, 8, 2, 8, width).transpose(1, 3, 0, 2, 4, 5).reshape(rows, width)

    parts = out.reshape(2, 2, 5, 8, 8, width).transpose(2, 0, 3, 1, 4, 5).reshape(5, 2, 8, 16, width)
    result_sent = parts[3:].astype(bf16)
    result_got = swap_side(result_sent)
    got = result_got.astype(f32)
    pair = jnp.stack(in_order(low_side, parts[:2], got), axis=2)
    pair = pair.reshape(2, 2, 16, 16, width).transpose(0, 2, 1, 3, 4).reshape(-1, width)
    shared = parts[2].transpose(1, 0, 2, 3).reshape(-1, width)
    result = either(
        low_side, jnp.concatenate([pair, shared], axis=0), jnp.concatenate([shared, pair], axis=0)
    )

    def crossing(mine, sib):
        return (mine.astype(f32) + swap_core(sib).astype(f32)).astype(bf16)

    def joined(mine, sib, got):
        return (mine.astype(f32) + swap_core(sib).astype(f32) + got.astype(f32)).astype(bf16)

    def turn_z(value, distance):
        return lax.ppermute(value, "z", [(i, (i + distance) % size_z) for i in range(size_z)])

    def y_sent(value):
        halves = value.reshape((2, -1) + value.shape[1:])
        kept = lax.dynamic_index_in_dim(halves, here_y, 0, keepdims=False)
        return kept, swap_y(lax.dynamic_index_in_dim(halves, 1 - here_y, 0, keepdims=False))

    def z_sent(kept, got):
        total = (kept.astype(f32) + got.astype(f32)).astype(bf16)
        parts = total.reshape((size_z, -1) + total.shape[1:])
        sent = [
            lax.dynamic_index_in_dim(parts, (here_z + k) % size_z, 0, keepdims=False)
            for k in range(size_z)
        ]
        return [sent[0]] + [turn_z(sent[k], k) for k in range(1, size_z)]

    def z_back(parts):
        total = sum(part.astype(f32) for part in parts).astype(bf16)
        return [total] + [turn_z(total, k) for k in range(1, size_z)]

    def y_back(parts):
        row = jnp.stack(parts[::-1] + parts[:0:-1])
        half = lax.dynamic_slice_in_dim(row, size_z - 1 - here_z, size_z, 0)
        half = half.reshape((-1,) + half.shape[2:])
        return half, swap_y(half)

    def both_quarters(half, got):
        full = jnp.concatenate(in_order(here_y == 0, half, got))
        other = jnp.concatenate(in_order(here_y == 0, swap_core(half), swap_core(got)))
        return in_order(first_core, full, other)

    def by_quarter(value):
        parts = value.reshape(2, -1, value.shape[-1])
        return parts[0], parts[1]

    collected, waiting, first_sums = [None, None], (result_sent,), ()
    sums = [{}, {}]
    steps = (y_sent, z_sent, z_back, y_back)

    def advance(trigger, *names):
        marks = []
        for name in names:
            value, step = sums[0][name]
            value = after_all(tuple(value), trigger)
            sums[0][name] = (steps[step](*value) if step < 2 else steps[step](value), step + 1)
            marks.append(sums[0][name][0][0])
        return marks

    def both_cores(value):
        return in_order(first_core, value, swap_core(value))

    for layer in (1, 0):
        shift_one, scale_one, gate_one, shift_two, scale_two, gate_two = [
            modulation[layer, number][None] for number in range(6)
        ]
        (
            x, turned, own_proj, far_proj, own_att, far_att, branch, middle, turned_two,
            own_pre, own_hidden, far_pre, far_hidden, branch_two, ublk, place,
        ) = saved[layer]
        gdb = (gate_two * g).astype(bf16)
        gate_two_grad = jnp.sum(g * branch_two, axis=0)

        def feed(own, r, *first):
            hidden, pre = (own_hidden, own_pre) if own else (far_hidden[r], far_pre[r])
            weights = (down_weight, up_weight) if own else (far_down[layer][r], far_up[layer][r])
            return feed_back(
                spots, layer, own, r, after(gdb, *first), hidden, pre, turned_two, *weights
            )

        far_sib = feed(False, 1, *waiting)
        far_mine = feed(False, 0, far_sib[0])
        far_down_sum, far_up_sum = crossing(far_mine[0], far_sib[0]), crossing(far_mine[1], far_sib[1])
        own_sib = feed(True, 1, far_down_sum, far_up_sum, *([result_got] if layer == 1 else []))
        down_got = swap_side(far_down_sum)
        own_mine = feed(True, 0, own_sib[0])
        far, own = (far_mine, far_sib), (own_mine, own_sib)
        grad_middle, grad_own, grad_far, own_out, far_out_grad, sums_two = join_back(
            spots, layer, [far[1][3], far[0][3], own[1][3], own[0][3]], g, middle, branch, own_att, far_att,
            output_weight, *far_out[layer], gate_one, scale_two,
        )
        down_sum = joined(own_mine[0], own_sib[0], down_got)
        up_got = swap_side(after(far_up_sum, down_got))

        far_grad, far_acc = attend_back(
            spots, 2, far_proj, after(grad_far, down_sum), ublk, place
        )
        in_mine, in_sib = in_grad(spots, turned, far_grad)
        own_grad, own_acc = attend_back(
            spots, 0, own_proj, after(grad_own, in_mine), ublk, place
        )
        far_in_sum = crossing(in_mine, in_sib)
        far_out_sum = crossing(*by_quarter(after(far_out_grad, in_mine)))
        up_sum = joined(own_mine[1], own_sib[1], up_got)
        in_mine, in_sib = in_grad(
            spots, after(turned, far_in_sum, far_out_sum, up_sum, *first_sums), own_grad
        )
        in_got, out_got = swap_side(far_in_sum), swap_side(far_out_sum)
        g, sums_one = project_back(
            spots, layer, own_grad, far_grad, in_weight, *far_in[layer], x,
            after(grad_middle, in_mine), scale_one,
        )
        out_sum = joined(*by_quarter(own_out), out_got)
        in_sum = joined(in_mine, in_sib, in_got)
        cut = in_sum.size // in_sum.shape[2]
        last = jnp.concatenate([part.reshape(-1, in_sum.shape[2]) for part in (in_sum, out_sum)])
        sums[layer]["last"] = ((last,), 0)
        if layer == 0:
            sums_one, g = after_all((sums_one, g), *advance(g, "last"))
            second_sums = lax.psum(after_all((down_sum, up_sum, first_last), *first_sums), chip_axes)
        table_rows = jnp.stack(
            [sums_one[0], sums_one[1], sums_two[2], sums_two[0], sums_two[1], gate_two_grad]
        )
        if layer == 1:
            parts = g.reshape(2, 2, 5, 8, 8, width).transpose(2, 0, 3, 1, 4, 5).reshape(5, 2, 128, width)
            kept = jnp.concatenate(
                [parts[:2].reshape(4, 128, width), either(low_side, parts[2, 0], parts[2, 1])[None]]
            )
            sent = jnp.concatenate(
                [parts[3:].reshape(4, 128, width), either(low_side, parts[2, 1], parts[2, 0])[None]]
            )
            got = swap_side(after(sent.astype(bf16), in_got, out_got)).astype(f32)
            g = jnp.stack(in_order(low_side, kept, got), axis=1).reshape(rows, width)
            first_sums, first_last = lax.psum((down_sum, up_sum), chip_axes), last
            waiting = (last,)
        rows_by_side = table_rows.reshape(6, 2, half)

        def packed(place, acc, pieces):
            return jnp.concatenate(
                [
                    lax.dynamic_index_in_dim(rows_by_side, place, 1, keepdims=False).reshape(-1),
                    table_grad(acc, *maps[layer]).reshape(-1),
                ]
                + [part.reshape(-1) for part in in_order(first_core, pieces[0][2], pieces[1][2])]
            )

        collected[layer] = (packed(side, own_acc, own), packed(1 - side, far_acc, far))

    small = jnp.concatenate([collected[0][0], collected[1][0]])
    small += swap_side(jnp.concatenate([collected[0][1], collected[1][1]]))
    spread = gather_dp(jnp.concatenate([small, activated.astype(f32)]))
    modulation_rows, offset_sums, bias_sums, start = [], [], [], 0
    for layer in range(2):
        modulation_rows.append(spread[:, start : start + 6 * half].reshape(-1, 6, half))
        start += 6 * half
        heads, levels = tables[layer].shape[0] // 2, tables[layer].shape[1]
        offset_sums.append(
            jnp.sum(spread[:, start : start + heads * levels], axis=0).reshape(heads, levels)
        )
        start += heads * levels
        bias_sums.append(jnp.sum(spread[:, start : start + up_bias.shape[1]], axis=0))
        start += up_bias.shape[1]
    modulation_rows = jnp.stack(modulation_rows).transpose(0, 2, 1, 3)

    parts = g.reshape(5, 2, 128, width)
    kept = lax.dynamic_index_in_dim(parts[4], side, 0, keepdims=False).reshape(8, 16, width)
    sent = lax.dynamic_index_in_dim(parts[4], 1 - side, 0, keepdims=False).reshape(8, 16, width)
    shared = jnp.stack(in_order(low_side, kept, swap_side(sent)), axis=1).reshape(-1, width)
    whole = parts[:4].reshape(2, 2, 16, 16, width).transpose(0, 2, 1, 3, 4).reshape(-1, width)
    grad_tokens = either(
        low_side, jnp.concatenate([whole, shared], axis=0), jnp.concatenate([shared, whole], axis=0)
    )

    for _ in range(3):
        advance(g, "last")
    quarters = []
    for layer in range(2):
        down_up = (second_sums[:2], first_sums)[layer]
        parts = {"down": both_cores(down_up[0]), "up": both_cores(down_up[1])}
        if layer == 0:
            parts["last"] = both_quarters(*sums[0]["last"][0])
        else:
            parts["last"] = both_cores(second_sums[2])
        quarters.append(
            (
                [part[:cut].reshape(in_sum.shape) for part in parts["last"]],
                [part[cut:].reshape(out_sum.shape) for part in parts["last"]],
                parts["up"],
                parts["down"],
            )
        )

    def pair_of(number, axis):
        return jnp.stack(
            [jnp.concatenate(quarters[layer][number], axis=axis).astype(f32) for layer in range(2)]
        )

    return (
        result,
        grad_tokens,
        modulation_back(spots, spread[:, start:], modulation_rows).transpose(0, 2, 1, 3),
        jnp.sum(modulation_rows, axis=2),
        pair_of(0, 2).transpose(0, 2, 1, 3),
        pair_of(1, 0),
        offset_sums[0],
        offset_sums[1],
        pair_of(2, 1),
        jnp.stack(bias_sums),
        pair_of(3, 0),
    )


def solution(mesh):
    chips, odd = divmod(mesh.shape["dp"], 2)
    if mesh.shape["mp"] == 2 and not odd and chips > 1 and chips & (chips - 1) == 0:
        dp, run = ("z", "y", "core"), per_device_pair
        mesh = Mesh(mesh.devices.reshape(-1, 2, 2, 2), dp + ("mp",))
    else:
        dp, run = ("dp",), per_device
    both = dp + ("mp",)
    return jax.shard_map(
        run,
        mesh=mesh,
        in_specs=(
            P(both, None),
            P(both, None),
            P(dp),
            P(dp),
            P(dp),
            P(),
            P(),
            P(None, None, None, "mp"),
            P(None, None, "mp"),
            P(None, None, None, "mp"),
            P(None, "mp", None),
            P("mp", None),
            P("mp", None),
            P(None, None, "mp"),
            P(None, "mp"),
            P(None, "mp", None),
        ),
        out_specs=(
            P(both, None),
            P(both, None),
            P(None, None, None, "mp"),
            P(None, None, "mp"),
            P(None, None, None, "mp"),
            P(None, "mp", None),
            P("mp", None),
            P("mp", None),
            P(None, None, "mp"),
            P(None, "mp"),
            P(None, "mp", None),
        ),
        check_vma=False,
    )
```
